512 devices in a mesh: ep: 128 (over z, y, core), tp: 4 (over x).
Axes of the slice: x: 4, y: 4, z: 16, core: 2. Of those that a mesh axis runs over, the one named last changes fastest.
Arguments:
- queries: bfloat16 [256, 128, 576], P('ep', 'tp'), may hold values from -40 to 40
- latent_cache: bfloat16 [256, 1024, 576], P('ep', 'tp'), may hold values from -4 to 4
- cache_lengths: int32 [256], P('ep'), may hold values from 128 to 1024, as said below
- moe_tokens: bfloat16 [4096, 3584], P('ep'), may hold values from -6 to 6
- expert_ids: int32 [4096, 8], P('ep'), may hold values from 0 to 127, all different within a row; in each aligned block of 32 rows (0 to 31, 32 to 63, ...) at most 4 rows name the same one
- gate_scores: float32 [4096, 8], P('ep'), may hold values from 0.05 to 1
- up_weight: bfloat16 [128, 3584, 1024], P('ep', None, 'tp'), may hold values from -0.09375 to 0.09375
- down_weight: bfloat16 [128, 1024, 3584], P('ep', 'tp'), may hold values from -0.1875 to 0.1875
Outputs:
- attention_out: bfloat16 [256, 128, 512], P('ep', 'tp')
- expert_mix: bfloat16 [4096, 3584], P('ep', 'tp')
The draws below stay inside these ranges and needn't reach their ends.
Inputs may be any that keep to these rules, and one draw needn't show every extreme that they name: `expert_ids`: in each aligned block of 32 rows (the rows of one device) no expert is named more than 4 times; the entries of a row differ. `cache_lengths`: some sequence has all 1024 positions valid.
All inputs are finite; a program needn't handle non-finite values.
Results may differ from the reference program's by a relative error of at most 0.017.
Values may be sent and summed in bfloat16 or wider, within the bound.
No kernel may reach another device: no remote copies, remote signals or barrier semaphores. Data moves between devices by JAX's collectives and lax.ppermute only.
A program may use at most 64 MiB of HBM per device.

```python
import math
import jax
import jax.numpy as jnp
import numpy as np
from jax import lax

D = 3584
HID = 1024
HEADS = 128
LATENT = 512
ROPE = 64
TOP = 8
CACHE = 1024
MOE_ROWS = 32
EXPERTS = 128
CAP = 4
ATT_TOTAL = 256
MOE_TOTAL = 4096
N_EP = 128
N_TP = 4


def latent_base(key):
    return jnp.clip(jax.random.normal(key, (ATT_TOTAL, CACHE, LATENT + ROPE), jnp.float32), -4.0, 4.0)


def draw_latent_cache(key, part):
    latents = latent_base(key)
    return latents.astype(jnp.bfloat16)


def draw_queries(key, part):
    key = jax.random.fold_in(key, 23)
    sampled = 0.5 * jax.random.normal(key, (ATT_TOTAL, HEADS, LATENT + ROPE), jnp.float32)
    return jnp.clip(sampled, -40.0, 40.0).astype(jnp.bfloat16)


def draw_cache_lengths(key, part):
    key = jax.random.fold_in(key, 37)
    sampled = jax.random.randint(key, (ATT_TOTAL,), max(4, CACHE // 8), CACHE + 1, jnp.int32)
    return sampled.at[0].set(CACHE)


def levels(key, shape, shards, low, high):
    loudness, own = 1.0, jax.random.fold_in(key, 6)
    for position, parts in shards:
        steps = jnp.exp(jax.random.uniform(jax.random.fold_in(own, position), (parts,), jnp.float32, low / len(shards), high / len(shards)))
        loudness = loudness * jnp.repeat(steps, shape[position] // parts).reshape([-1 if axis == position else 1 for axis in range(len(shape))])
    return loudness


def deal_out(rng, own, number, rows, amount, top, limit, slope):
    ranking = jax.random.permutation(rng, amount)
    heavy_load, usual = load_shares(amount, rows * top, limit, slope, True), load_shares(amount, rows * top, limit, slope, False)
    places = jnp.arange(amount)

    def named(sizes, rotation):
        used = int((sizes > 0).sum())
        fixed = max(1, used // 4)
        passed = fixed + (places - fixed + rotation * (used - fixed)) % max(1, amount - fixed)
        return jnp.zeros((amount,), jnp.int32).at[ranking[jnp.where(places < fixed, places, passed)]].set(jnp.asarray(sizes, jnp.int32))

    sizes = jnp.where(number % 4 == 0, named(heavy_load, number // 4), named(usual, number - number // 4 - 1))
    mixed = jax.random.permutation(jax.random.fold_in(own, 3), amount)
    donor, taker = mixed[0:amount // 2 * 2:2], mixed[1:amount // 2 * 2:2]
    margin = jnp.minimum(sizes[donor] - 1, limit - sizes[taker]) // 2
    margin = jnp.where((donor == ranking[0]) | (taker == ranking[0]) | (sizes[taker] == 0), 0, jnp.maximum(margin, 0))
    passed = jax.random.randint(jax.random.fold_in(own, 4), (amount // 2,), 0, 1 << 20) % (margin + 1)
    sizes = sizes.at[donor].add(-passed).at[taker].add(passed)
    items = jnp.searchsorted(jnp.cumsum(sizes), jnp.arange(rows * top), side="right").astype(jnp.int32)
    table = items.reshape(top, rows).T
    table = table[jax.random.permutation(jax.random.fold_in(own, 1), rows)]
    rotation = jax.random.randint(jax.random.fold_in(own, 2), (rows, 1), 0, top)
    return jnp.take_along_axis(table, (jnp.arange(top)[None, :] + rotation) % top, axis=1)


def load_shares(count, total, most, slope, full):
    portions = [(1 << 20) // math.isqrt(rank ** slope) + 1 for rank in range(1, count + 1)]
    largest = most if full else min(most, max(-(-total // count), total * portions[0] // sum(portions)))
    least = 1 if total - largest >= count - 1 else 0
    holding, surplus = [largest] + [least] * (count - 1), total - largest - least * (count - 1)
    while surplus > 0:
        movable = [i for i in range(1, count) if holding[i] < largest] or [i for i in range(1, count) if holding[i] < most]
        pool, remaining = sum([portions[i] for i in movable]), surplus
        for i in movable:
            more = min(most - holding[i], max(1, remaining * portions[i] // pool), surplus)
            holding[i] = holding[i] + more
            surplus = surplus - more
    return np.array(holding)


def centred(rng, extent, spread, reach, cuts=(), held_as=jnp.bfloat16):
    array = jax.random.normal(rng, extent, jnp.float32) * spread
    if len(cuts) > 0:
        array = levels(rng, extent, cuts, -0.22, 0.18) * array
    return jnp.clip(array, min=-reach, max=reach).astype(held_as)


def setup_inputs(seed: int = 0) -> dict:
    key_list = jax.random.split(jax.random.key(seed), 9)
    queries = draw_queries(jax.random.fold_in(key_list[8], 71), 0)
    latent_cache = draw_latent_cache(jax.random.fold_in(key_list[8], 71), 0)
    cache_lengths = draw_cache_lengths(jax.random.fold_in(key_list[8], 71), 0)
    moe_tokens = centred(key_list[3], (MOE_TOTAL, D), 1.0, 6.0, ((0, 128),))
    expert_ids_keys = jax.random.split(jax.random.fold_in(key_list[4], 1), MOE_TOTAL // MOE_ROWS)
    expert_ids_turns = jax.random.permutation(jax.random.fold_in(key_list[4], 3), MOE_TOTAL // MOE_ROWS)
    expert_ids = jax.vmap(lambda own, number: deal_out(jax.random.fold_in(key_list[4], 2), own, number, MOE_ROWS, EXPERTS, TOP, CAP, 2))(expert_ids_keys, expert_ids_turns).reshape((MOE_TOTAL, TOP))
    gate_scores = jnp.clip(jnp.exp(math.log(1.0) - 2.9957323 * jax.random.uniform(key_list[5], (MOE_TOTAL, TOP), jnp.float32) ** levels(key_list[5], (MOE_TOTAL, TOP), ((0, 128),), -0.2, 0.2)), 0.05, 1.0)
    up_weight = centred(key_list[6], (EXPERTS, D, HID), D ** -0.5, 0.09375, ((0, 128), (2, 4)))
    down_weight = centred(key_list[7], (EXPERTS, HID, D), HID ** -0.5, 0.1875, ((0, 128), (1, 4)))
    return dict(queries=queries, latent_cache=latent_cache, cache_lengths=cache_lengths, moe_tokens=moe_tokens, expert_ids=expert_ids, gate_scores=gate_scores, up_weight=up_weight, down_weight=down_weight)


SCALE = 192.0 ** -0.5
ROUTE_SCALE = 2.5
NEGATIVE = -1e30


def attend(queries, latent_cache, cache_lengths):
    scores = jnp.einsum("rhc,rnc->rhn", queries.astype(jnp.float32), latent_cache.astype(jnp.float32)) * SCALE
    positions = jnp.arange(CACHE, dtype=jnp.int32)
    visible = positions[None, None, :] < cache_lengths[:, None, None]
    scores = jnp.where(visible, scores, NEGATIVE)
    peak = jnp.max(scores, axis=-1, keepdims=True)
    probs = jnp.where(visible, jnp.exp(scores - peak), 0.0)
    summed = jnp.sum(probs, axis=-1)
    rounded = lax.optimization_barrier(probs.astype(jnp.bfloat16)).astype(jnp.float32)
    values = latent_cache[:, :, :LATENT].astype(jnp.float32)
    weighted = jnp.einsum("rhn,rnc->rhc", rounded, values)
    return (weighted / summed[..., None]).astype(jnp.bfloat16)


def expert_apply(picked_rows, up_matrix, down_matrix):
    preact = jnp.dot(picked_rows, up_matrix, preferred_element_type=jnp.float32)
    hidden = jax.nn.silu(preact).astype(jnp.bfloat16)
    group_width = HID // N_TP
    summed = jnp.zeros((picked_rows.shape[0], D), jnp.float32)
    for group_index in range(N_TP):
        low = group_index * group_width
        partial_value = jnp.dot(hidden[:, low:low + group_width], down_matrix[low:low + group_width], preferred_element_type=jnp.float32)
        partial_value = lax.optimization_barrier(partial_value.astype(jnp.bfloat16)).astype(jnp.float32)
        summed = summed + partial_value
    return summed.astype(jnp.bfloat16)


def mix_experts(moe_tokens, expert_ids, gate_scores, up_weight, down_weight):
    slot_total = N_EP * CAP
    flat_ids = expert_ids.reshape(-1)
    route_weights = gate_scores / jnp.sum(gate_scores, axis=1, keepdims=True) * ROUTE_SCALE
    flat_weight = route_weights.reshape(-1)

    def one_expert(mixed_rows, expert):
        hits = flat_ids == expert
        chosen = jnp.nonzero(hits, size=slot_total, fill_value=0)[0].astype(jnp.int32)
        occupied = jnp.arange(slot_total, dtype=jnp.int32) < jnp.sum(hits.astype(jnp.int32))
        sources = (chosen // TOP).astype(jnp.int32)
        output = expert_apply(moe_tokens[sources], up_weight[expert], down_weight[expert]).astype(jnp.float32)
        scaled = jnp.where(occupied[:, None], flat_weight[chosen][:, None] * output, 0.0)
        return mixed_rows.at[sources].add(scaled), None

    start_rows = jnp.zeros((MOE_TOTAL, D), jnp.float32)
    mixed_rows, unused = lax.scan(one_expert, start_rows, jnp.arange(EXPERTS, dtype=jnp.int32))
    return mixed_rows.astype(jnp.bfloat16)


def reference(queries, latent_cache, cache_lengths, moe_tokens, expert_ids, gate_scores, up_weight, down_weight):
    attention_out = attend(queries, latent_cache, cache_lengths)
    expert_mix = mix_experts(moe_tokens, expert_ids, gate_scores, up_weight, down_weight)
    return (attention_out, expert_mix)
```

```python
import functools

import jax
import jax.numpy as jnp
from jax import lax
from jax.experimental import pallas as pl
from jax.experimental.pallas import tpu as pltpu
from jax.sharding import Mesh, PartitionSpec as P

LATENT = 512
TOP = 8
CAP = 4
SCALE = 192.0 ** (-0.5)
ROUTE_SCALE = 2.5
NEGATIVE = -1e30
LANES = 128
VMEM = 32 << 20
INSIDE = pl.BlockSpec(memory_space=pltpu.VMEM)
OUTSIDE = pl.BlockSpec(memory_space=pl.ANY)

EP = ("zh", "zl", "y", "c")
NEAR = ("zl", "y", "c")
FAR = "zh"
BF = jnp.bfloat16


def cost(flops, *arrays):
    size = sum(a.size * a.dtype.itemsize for a in arrays)
    return pl.CostEstimate(flops=flops, bytes_accessed=size, transcendentals=0)


def attend_kernel(place_ref, q0, q1, q2, q3, cache_ref, out_ref):
    r = pl.program_id(0)
    keys = cache_ref[0]
    asked = [q[:, : keys.shape[0]] for q in (q0, q1, q2, q3)]
    count = asked[0].shape[0]
    scores = jnp.dot(jnp.concatenate(asked, axis=0), keys, preferred_element_type=jnp.float32) * SCALE
    positions = place_ref[2] + lax.broadcasted_iota(jnp.int32, scores.shape, 1)
    visible = positions < place_ref[r]
    scores = jnp.where(visible, scores, NEGATIVE)
    peak = jnp.max(scores, axis=1, keepdims=True)
    weights = jnp.where(visible, jnp.exp(scores - peak), 0.0)
    total = jnp.sum(weights, axis=1, keepdims=True)
    mixed = lax.dot_general(
        weights.astype(BF), keys[:LATENT], (((1,), (1,)), ((), ())), preferred_element_type=jnp.float32
    )
    mean = (mixed / jnp.where(total > 0.0, total, 1.0)).astype(BF)
    lane = lax.broadcasted_iota(jnp.int32, (scores.shape[0], LANES), 1)
    stats = jnp.zeros((scores.shape[0], LANES), jnp.float32)
    for first, value in ((0, peak), (3, total)):
        for i in range(3):
            part = value.astype(BF).astype(jnp.float32)
            stats = jnp.where(lane == first + i, part, stats)
            value = value - part
    stats = stats.astype(BF)
    for k in range(4):
        out_ref[k, 0, :, :LATENT] = mean[k * count : (k + 1) * count]
        out_ref[k, 0, :, LATENT:] = stats[k * count : (k + 1) * count]


def attend_own(asked, starts, count, cache, cache_lengths, first):
    keys = jnp.swapaxes(cache, 1, 2)
    rows, channels, positions = keys.shape
    out = jax.ShapeDtypeStruct((len(asked), rows, count, LATENT + LANES), BF)
    place = jnp.concatenate([cache_lengths, first.reshape(1).astype(jnp.int32)])

    def queries(array, start):
        return pl.BlockSpec((count, array.shape[1]), lambda r, place: (start // count + r, 0))

    return pl.pallas_call(
        attend_kernel,
        out_shape=out,
        grid_spec=pltpu.PrefetchScalarGridSpec(
            num_scalar_prefetch=1,
            grid=(rows,),
            in_specs=[queries(a, i) for a, i in zip(asked, starts)]
            + [pl.BlockSpec((1, channels, positions), lambda r, place: (r, 0, 0))],
            out_specs=pl.BlockSpec((len(asked), 1, count, LATENT + LANES), lambda r, place: (0, r, 0, 0)),
        ),
        compiler_params=pltpu.CompilerParams(vmem_limit_bytes=VMEM),
        cost_estimate=cost(4 * rows * 4 * count * channels * positions, cache, out),
        name="attend_own",
    )(place, *asked, keys)


def merge(parts):
    means = [p[..., :LATENT].astype(jnp.float32) for p in parts]
    stats = [p[..., LATENT : LATENT + 6].astype(jnp.float32) for p in parts]
    peaks = [q[..., 0] + q[..., 1] + q[..., 2] for q in stats]
    totals = [q[..., 3] + q[..., 4] + q[..., 5] for q in stats]
    peak = jnp.max(jnp.stack(peaks), axis=0)
    shares = [t * jnp.exp(p - peak) for p, t in zip(peaks, totals)]
    whole = sum(shares)
    return sum((s / whole)[..., None] * m for s, m in zip(shares, means)).astype(BF)


def routing_columns(expert_ids, gate_scores):
    route = gate_scores / jnp.sum(gate_scores, axis=1, keepdims=True) * ROUTE_SCALE
    high = lax.reduce_precision(route, 8, 7)
    low = route - high
    rows = expert_ids.shape[0]
    parts = [expert_ids.astype(BF), high.astype(BF), low.astype(BF)]
    return jnp.concatenate(parts + [jnp.zeros((rows, LANES - 3 * TOP), BF)], axis=1)


def place_kernel(first_ref, packed_ref, out_ref, held, sems, *, rows, experts, slots):
    total, wide = packed_ref.shape
    cols = wide - LANES
    ids = packed_ref[:, cols:].astype(jnp.float32).T
    own = (first_ref[0] + lax.broadcasted_iota(jnp.int32, (experts, total), 0)).astype(jnp.float32)
    named = own == ids[0:1]
    for k in range(1, TOP):
        named = named | (own == ids[k : k + 1])
    before, after = (lax.broadcasted_iota(jnp.int32, (total, total), d) for d in (0, 1))
    earlier = (before < after) & (before // rows == after // rows)
    rank = jnp.dot(
        jnp.where(named, 1.0, 0.0).astype(BF),
        jnp.where(earlier, 1.0, 0.0).astype(BF),
        preferred_element_type=jnp.float32,
    )
    block = lax.broadcasted_iota(jnp.int32, (experts, total), 1) // rows
    slot = jnp.where(named, rank + (block * CAP).astype(jnp.float32), -1.0)
    place = lax.broadcasted_iota(jnp.int32, (experts, slots, total), 1).astype(jnp.float32)
    put = jnp.where(jnp.broadcast_to(slot[:, None, :], place.shape) == place, 1.0, 0.0)
    put = put.reshape(experts * slots, total).astype(BF)
    step = held.shape[0] // sems.shape[0]
    copies = []
    for i in range(sems.shape[0]):
        part = pl.ds(i * step, step)
        moved = jnp.dot(put[i * step : (i + 1) * step], packed_ref[:, :cols], preferred_element_type=jnp.float32)
        held[part] = moved.astype(BF)
        copies.append(pltpu.make_async_copy(held.at[part], out_ref.at[part], sems.at[i]))
        copies[-1].start()
    for copy in copies:
        copy.wait()


def placed_rows(first, packed, rows, experts, slots):
    total, wide = packed.shape
    out = jax.ShapeDtypeStruct((experts * slots, wide - LANES), BF)
    return pl.pallas_call(
        functools.partial(place_kernel, rows=rows, experts=experts, slots=slots),
        out_shape=out,
        in_specs=[pl.BlockSpec(memory_space=pltpu.SMEM), INSIDE],
        out_specs=OUTSIDE,
        scratch_shapes=[pltpu.VMEM(out.shape, BF), pltpu.SemaphoreType.DMA((4,))],
        compiler_params=pltpu.CompilerParams(vmem_limit_bytes=VMEM),
        cost_estimate=cost(2 * out.size * total, packed, out),
        name="placed_rows",
    )(first.reshape(1), packed)


def shares(columns, rows, first, experts, blocks):
    ids = columns[:, :TOP].astype(jnp.float32)
    high = columns[:, TOP : 2 * TOP].astype(jnp.float32)
    low = columns[:, 2 * TOP : 3 * TOP].astype(jnp.float32)
    own = (first + jnp.arange(experts, dtype=jnp.int32)).astype(jnp.float32)
    hit = ids[:, :, None] == own[None, None, :]
    named = jnp.any(hit, axis=1)
    w_high = jnp.sum(jnp.where(hit, high[:, :, None], 0.0), axis=1)
    w_low = jnp.sum(jnp.where(hit, low[:, :, None], 0.0), axis=1)
    total = rows * blocks
    t = jnp.arange(total, dtype=jnp.int32)
    before = (t[None, :] < t[:, None]) & (t[None, :] // rows == t[:, None] // rows)
    rank = jnp.dot(before.astype(BF), named.astype(BF), preferred_element_type=jnp.float32)
    slot = rank + ((t // rows) * CAP).astype(jnp.float32)[:, None]
    slot = jnp.where(named, slot, -1.0)
    slots = jnp.arange(blocks * CAP, dtype=jnp.int32).astype(jnp.float32)
    take = slot[:, :, None] == slots[None, None, :]
    c_high = jnp.where(take, w_high[:, :, None], 0.0).astype(BF).reshape(total, -1)
    c_low = jnp.where(take, w_low[:, :, None], 0.0).astype(BF).reshape(total, -1)
    return jnp.concatenate([c_high, c_low], axis=0)


def up_kernel(rows_ref, weight_ref, out_ref, held, sems):
    copies = []
    for j in range(weight_ref.shape[0]):
        held[j] = jnp.dot(rows_ref[...], weight_ref[j], preferred_element_type=jnp.float32).astype(BF)
        copies.append(pltpu.make_async_copy(held.at[j], out_ref.at[j], sems.at[j]))
        copies[-1].start()
    for copy in copies:
        copy.wait()


def up_parts(rows, weight):
    groups, depth, width = weight.shape
    count = rows.shape[0]
    out = jax.ShapeDtypeStruct((groups, count, width), BF)
    return pl.pallas_call(
        up_kernel,
        out_shape=out,
        in_specs=[INSIDE, INSIDE],
        out_specs=OUTSIDE,
        scratch_shapes=[pltpu.VMEM(out.shape, BF), pltpu.SemaphoreType.DMA((groups,))],
        compiler_params=pltpu.CompilerParams(vmem_limit_bytes=VMEM),
        cost_estimate=cost(2 * count * depth * width * groups, rows, weight, out),
        name="up_parts",
    )(rows, weight)


def hidden_kernel(part_ref, out_ref, held, sems):
    groups, count, _ = part_ref.shape
    step = count // sems.shape[0]
    copies = []
    for i in range(sems.shape[0]):
        rows = pl.ds(i * step, step)
        value = part_ref[0, rows].astype(jnp.float32)
        for j in range(1, groups):
            value = value + part_ref[j, rows].astype(jnp.float32)
        held[rows] = (value / (1.0 + jnp.exp(-value))).astype(BF)
        for j in range(groups):
            copies.append(pltpu.make_async_copy(held.at[rows], out_ref.at[j, rows], sems.at[i, j]))
            copies[-1].start()
    for copy in copies:
        copy.wait()


def hidden_copies(part):
    return pl.pallas_call(
        hidden_kernel,
        out_shape=jax.ShapeDtypeStruct(part.shape, BF),
        in_specs=[INSIDE],
        out_specs=OUTSIDE,
        scratch_shapes=[pltpu.VMEM(part.shape[1:], BF), pltpu.SemaphoreType.DMA((2, part.shape[0]))],
        compiler_params=pltpu.CompilerParams(vmem_limit_bytes=VMEM),
        cost_estimate=cost(10 * part.size, part, part),
        name="hidden_copies",
    )(part)


def down_kernel(x_ref, hidden_ref, w0, w1, w2a, w2b, w3, out_ref, held, sems):
    groups = hidden_ref.shape[0]
    step = held.shape[0] // sems.shape[0]
    place = [lax.rem(x_ref[0] + k, groups) for k in range(groups)]
    copies = []

    def dot(left, right):
        return jnp.dot(left, right, preferred_element_type=jnp.float32)

    for i in range(sems.shape[0]):
        rows = pl.ds(i * step, step)
        total = dot(hidden_ref[place[0], rows], w0[...])
        total = total + dot(hidden_ref[place[1], rows], w1[...])
        total = total + dot(hidden_ref[place[3], rows], w3[...])
        far = hidden_ref[place[2], rows]
        depth = w0.shape[0] // 2
        total = total + dot(far[:, :depth], w2a[:depth, :])
        total = total + dot(far[:, depth:], w2b[:depth, :])
        held[rows] = total.astype(BF)
        copies.append(pltpu.make_async_copy(held.at[rows], out_ref.at[rows], sems.at[i]))
        copies[-1].start()
    for copy in copies:
        copy.wait()


def down_rows(x, hidden, own, after, far_low, far_high, before):
    out = jax.ShapeDtypeStruct((hidden.shape[1], own.shape[1]), BF)
    return pl.pallas_call(
        down_kernel,
        out_shape=out,
        in_specs=[pl.BlockSpec(memory_space=pltpu.SMEM)] + [INSIDE] * 6,
        out_specs=OUTSIDE,
        scratch_shapes=[pltpu.VMEM(out.shape, BF), pltpu.SemaphoreType.DMA((4,))],
        compiler_params=pltpu.CompilerParams(vmem_limit_bytes=VMEM),
        cost_estimate=cost(2 * hidden.size * own.shape[1], hidden, own, own, own, own, out),
        name="down_rows",
    )(x.reshape(1), hidden, own, after, far_low, far_high, before)


def shift(array, by, tp):
    return lax.ppermute(array, "tp", [(i, (i + by) % tp) for i in range(tp)])


def shards(queries, latent_cache, cache_lengths, moe_tokens, expert_ids, gate_scores, up_weight, down_weight):
    tp = lax.axis_size("tp")
    x = lax.axis_index("tp")
    rows, width = moe_tokens.shape
    cols = width // tp
    group = up_weight.shape[2]
    near = lax.axis_size(NEAR)
    far = lax.axis_size(FAR)
    slots = far * CAP

    up = lax.all_to_all(up_weight[0].reshape(tp, cols, group), "tp", 0, 0, tiled=True)

    mine = lax.dynamic_slice_in_dim(moe_tokens, x * cols, cols, 1)
    packed = jnp.concatenate([mine, routing_columns(expert_ids, gate_scores)], axis=1)
    packed = lax.all_gather(packed, FAR, axis=0, tiled=True)
    packed, up = lax.optimization_barrier((packed, up))
    first = lax.axis_index(FAR) * near
    outgoing = placed_rows(first, packed, rows, near, slots)

    weight = down_weight[0]
    half = group // 2
    held = queries.reshape(-1, queries.shape[2])
    ask = jnp.pad(held, ((0, 0), (0, cols - held.shape[1])))

    def columns_for(k, low, high):
        return lax.dynamic_slice_in_dim(weight[low:high], (x + k) % tp * cols, cols, 1)

    right = shift(jnp.concatenate([columns_for(2, 0, half), ask], axis=0), 1, tp)
    left = shift(jnp.concatenate([columns_for(2, half, group), ask], axis=0), tp - 1, tp)
    before = shift(columns_for(1, 0, group), 1, tp)
    after = shift(columns_for(tp - 1, 0, group), tp - 1, tp)
    far_right, far_left = shift(right, 1, tp), shift(left, tp - 1, tp)
    received = lax.all_to_all(outgoing.reshape(near, slots, cols), NEAR, 0, 0, tiled=True)
    received, right, left, before, after, far_right, far_left = lax.optimization_barrier(
        (received.reshape(near * slots, cols), right, left, before, after, far_right, far_left)
    )
    take = shares(packed[:, cols:], rows, first, near, far)

    part = lax.all_to_all(up_parts(received, up), "tp", 0, 0, tiled=True)
    hidden = lax.all_to_all(hidden_copies(part), "tp", 0, 0, tiled=True)

    asked, starts = [held, left, far_right, right], [0, half, half, half]
    first = x * latent_cache.shape[1]
    own = attend_own(asked, starts, queries.shape[1], latent_cache, cache_lengths, first)
    hidden, own = lax.optimization_barrier((hidden, own))
    shared = [own[0]] + [shift(own[k], k, tp) for k in range(1, tp)]
    output = down_rows(x, hidden, columns_for(0, 0, group), after, far_right, far_left, before)

    returned = lax.all_to_all(output.reshape(near, slots, cols), NEAR, 0, 0, tiled=True)
    returned, shared = lax.optimization_barrier((returned, shared))
    mixed = jnp.dot(take, returned.reshape(near * slots, cols), preferred_element_type=jnp.float32)
    mixed = (mixed[: far * rows] + mixed[far * rows :]).astype(BF).reshape(far, rows, cols)
    mixed = lax.all_to_all(mixed, FAR, 0, 0, tiled=True)
    attention_out = merge(shared)
    expert_mix = jnp.sum(mixed.astype(jnp.float32), axis=0).astype(BF)
    return (attention_out, expert_mix)


def solution(mesh):
    devices = mesh.devices
    split = Mesh(devices.reshape(4, 4, 4, 2, devices.shape[1]), EP + ("tp",))
    placed = (
        P(EP, "tp", None),
        P(EP, "tp", None),
        P(EP),
        P(EP, None),
        P(EP, None),
        P(EP, None),
        P(EP, None, "tp"),
        P(EP, "tp", None),
    )
    return jax.shard_map(
        shards,
        mesh=split,
        in_specs=placed,
        out_specs=(P(EP, "tp", None), P(EP, "tp")),
        check_vma=False,
    )
```

```python
import functools

import jax
import jax.numpy as jnp
from jax import lax
from jax.experimental import pallas as pl
from jax.experimental.pallas import tpu as pltpu
from jax.sharding import Mesh, PartitionSpec as P

LATENT = 512
TOP = 8
CAP = 4
SCALE = 192.0 ** (-0.5)
ROUTE_SCALE = 2.5
NEGATIVE = -1e30
LANES = 128
VMEM = 12 << 20
INSIDE = pl.BlockSpec(memory_space=pltpu.VMEM)
OUTSIDE = pl.BlockSpec(memory_space=pltpu.HBM)

EP = ("zh", "zl", "y", "c")
NEAR = ("zl", "y", "c")
FAR = "zh"
BF = jnp.bfloat16


def cost(flops, *arrays):
    size = sum(a.size * a.dtype.itemsize for a in arrays)
    return pl.CostEstimate(flops=flops, bytes_accessed=size, transcendentals=0)


def attend_kernel(place_ref, q0, q1, q2, q3, cache_ref, out_ref):
    r = pl.program_id(0)
    keys = cache_ref[0]
    asked = [q[0] for q in (q0, q1, q2, q3)]
    count = asked[0].shape[0]
    scores = jnp.dot(jnp.concatenate(asked, axis=0), keys, preferred_element_type=jnp.float32) * SCALE
    positions = place_ref[2] + lax.broadcasted_iota(jnp.int32, scores.shape, 1)
    visible = positions < place_ref[r]
    scores = jnp.where(visible, scores, NEGATIVE)
    peak = jnp.max(scores, axis=1, keepdims=True)
    weights = jnp.where(visible, jnp.exp(scores - peak), 0.0)
    total = jnp.sum(weights, axis=1, keepdims=True)
    mixed = lax.dot_general(
        weights.astype(BF), keys[:LATENT], (((1,), (1,)), ((), ())), preferred_element_type=jnp.float32
    )
    mean = (mixed / jnp.where(total > 0.0, total, 1.0)).astype(BF)
    lane = lax.broadcasted_iota(jnp.int32, (scores.shape[0], LANES), 1)
    stats = jnp.zeros((scores.shape[0], LANES), jnp.float32)
    for first, value in ((0, peak), (3, total)):
        for i in range(3):
            part = value.astype(BF).astype(jnp.float32)
            stats = jnp.where(lane == first + i, part, stats)
            value = value - part
    stats = stats.astype(BF)
    for k in range(4):
        out_ref[k, 0, :, :LATENT] = mean[k * count : (k + 1) * count]
        out_ref[k, 0, :, LATENT:] = stats[k * count : (k + 1) * count]


def attend_own(asked, cache, cache_lengths, first):
    keys = jnp.swapaxes(cache, 1, 2)
    count = asked[0].shape[1]
    rows, channels, positions = keys.shape
    out = jax.ShapeDtypeStruct((len(asked), rows, count, LATENT + LANES), BF)
    place = jnp.concatenate([cache_lengths, first.reshape(1).astype(jnp.int32)])
    return pl.pallas_call(
        attend_kernel,
        out_shape=out,
        grid_spec=pltpu.PrefetchScalarGridSpec(
            num_scalar_prefetch=1,
            grid=(rows,),
            in_specs=[pl.BlockSpec((1, count, channels), lambda r, place: (r, 0, 0))] * len(asked)
            + [pl.BlockSpec((1, channels, positions), lambda r, place: (r, 0, 0))],
            out_specs=pl.BlockSpec((len(asked), 1, count, LATENT + LANES), lambda r, place: (0, r, 0, 0)),
        ),
        compiler_params=pltpu.CompilerParams(vmem_limit_bytes=VMEM),
        cost_estimate=cost(4 * rows * 4 * count * channels * positions, cache, out),
        name="attend_own",
    )(place, *asked, keys)


def merge(parts):
    means = [p[..., :LATENT].astype(jnp.float32) for p in parts]
    stats = [p[..., LATENT : LATENT + 6].astype(jnp.float32) for p in parts]
    peaks = [q[..., 0] + q[..., 1] + q[..., 2] for q in stats]
    totals = [q[..., 3] + q[..., 4] + q[..., 5] for q in stats]
    peak = jnp.max(jnp.stack(peaks), axis=0)
    shares = [t * jnp.exp(p - peak) for p, t in zip(peaks, totals)]
    whole = sum(shares)
    return sum((s / whole)[..., None] * m for s, m in zip(shares, means)).astype(BF)


def routing_columns(expert_ids, gate_scores):
    route = gate_scores / jnp.sum(gate_scores, axis=1, keepdims=True) * ROUTE_SCALE
    high = lax.reduce_precision(route, 8, 7)
    low = route - high
    rows = expert_ids.shape[0]
    parts = [expert_ids.astype(BF), high.astype(BF), low.astype(BF)]
    return jnp.concatenate(parts + [jnp.zeros((rows, LANES - 3 * TOP), BF)], axis=1)


def place_kernel(first_ref, packed_ref, out_ref, held, sems, *, rows, experts, slots):
    total, wide = packed_ref.shape
    cols = wide - LANES
    ids = packed_ref[:, cols:].astype(jnp.float32).T
    own = (first_ref[0] + lax.broadcasted_iota(jnp.int32, (experts, total), 0)).astype(jnp.float32)
    named = own == ids[0:1]
    for k in range(1, TOP):
        named = named | (own == ids[k : k + 1])
    before, after = (lax.broadcasted_iota(jnp.int32, (total, total), d) for d in (0, 1))
    earlier = (before < after) & (before // rows == after // rows)
    rank = jnp.dot(
        jnp.where(named, 1.0, 0.0).astype(BF),
        jnp.where(earlier, 1.0, 0.0).astype(BF),
        preferred_element_type=jnp.float32,
    )
    block = lax.broadcasted_iota(jnp.int32, (experts, total), 1) // rows
    slot = jnp.where(named, rank + (block * CAP).astype(jnp.float32), -1.0)
    place = lax.broadcasted_iota(jnp.int32, (experts, slots, total), 1).astype(jnp.float32)
    put = jnp.where(jnp.broadcast_to(slot[:, None, :], place.shape) == place, 1.0, 0.0)
    put = put.reshape(experts * slots, total).astype(BF)
    step = held.shape[0] // sems.shape[0]
    copies = []
    for i in range(sems.shape[0]):
        part = pl.ds(i * step, step)
        moved = jnp.dot(put[i * step : (i + 1) * step], packed_ref[:, :cols], preferred_element_type=jnp.float32)
        held[part] = moved.astype(BF)
        copies.append(pltpu.make_async_copy(held.at[part], out_ref.at[part], sems.at[i]))
        copies[-1].start()
    for copy in copies:
        copy.wait()


def placed_rows(first, packed, rows, experts, slots):
    total, wide = packed.shape
    out = jax.ShapeDtypeStruct((experts * slots, wide - LANES), BF)
    return pl.pallas_call(
        functools.partial(place_kernel, rows=rows, experts=experts, slots=slots),
        out_shape=out,
        in_specs=[pl.BlockSpec(memory_space=pltpu.SMEM), INSIDE],
        out_specs=OUTSIDE,
        scratch_shapes=[pltpu.VMEM(out.shape, BF), pltpu.SemaphoreType.DMA((4,))],
        compiler_params=pltpu.CompilerParams(vmem_limit_bytes=VMEM),
        cost_estimate=cost(2 * out.size * total, packed, out),
        name="placed_rows",
    )(first.reshape(1), packed)


def shares(columns, rows, first, experts, blocks):
    ids = columns[:, :TOP].astype(jnp.float32)
    high = columns[:, TOP : 2 * TOP].astype(jnp.float32)
    low = columns[:, 2 * TOP : 3 * TOP].astype(jnp.float32)
    own = (first + jnp.arange(experts, dtype=jnp.int32)).astype(jnp.float32)
    hit = ids[:, :, None] == own[None, None, :]
    named = jnp.any(hit, axis=1)
    w_high = jnp.sum(jnp.where(hit, high[:, :, None], 0.0), axis=1)
    w_low = jnp.sum(jnp.where(hit, low[:, :, None], 0.0), axis=1)
    total = rows * blocks
    t = jnp.arange(total, dtype=jnp.int32)
    before = (t[None, :] < t[:, None]) & (t[None, :] // rows == t[:, None] // rows)
    rank = jnp.dot(before.astype(BF), named.astype(BF), preferred_element_type=jnp.float32)
    slot = rank + ((t // rows) * CAP).astype(jnp.float32)[:, None]
    slot = jnp.where(named, slot, -1.0)
    slots = jnp.arange(blocks * CAP, dtype=jnp.int32).astype(jnp.float32)
    take = slot[:, :, None] == slots[None, None, :]
    c_high = jnp.where(take, w_high[:, :, None], 0.0).astype(BF).reshape(total, -1)
    c_low = jnp.where(take, w_low[:, :, None], 0.0).astype(BF).reshape(total, -1)
    return jnp.concatenate([c_high, c_low], axis=0)


def up_kernel(rows_ref, weight_ref, out_ref):
    for j in range(weight_ref.shape[0]):
        out_ref[j] = jnp.dot(rows_ref[...], weight_ref[j], preferred_element_type=jnp.float32).astype(BF)


def up_parts(rows, weight):
    groups, depth, width = weight.shape
    count = rows.shape[0]
    out = jax.ShapeDtypeStruct((groups, count, width), BF)
    return pl.pallas_call(
        up_kernel,
        out_shape=out,
        in_specs=[INSIDE, INSIDE],
        out_specs=INSIDE,
        compiler_params=pltpu.CompilerParams(vmem_limit_bytes=VMEM),
        cost_estimate=cost(2 * count * depth * width * groups, rows, weight, out),
        name="up_parts",
    )(rows, weight)


def hidden_kernel(part_ref, out_ref):
    groups, count, _ = part_ref.shape
    step = count // 4
    for i in range(4):
        rows = pl.ds(i * step, step)
        value = part_ref[0, rows].astype(jnp.float32)
        for j in range(1, groups):
            value = value + part_ref[j, rows].astype(jnp.float32)
        value = (value / (1.0 + jnp.exp(-value))).astype(BF)
        for j in range(groups):
            out_ref[j, rows] = value


def hidden_copies(part):
    return pl.pallas_call(
        hidden_kernel,
        out_shape=jax.ShapeDtypeStruct(part.shape, BF),
        in_specs=[INSIDE],
        out_specs=INSIDE,
        compiler_params=pltpu.CompilerParams(vmem_limit_bytes=VMEM),
        cost_estimate=cost(10 * part.size, part, part),
        name="hidden_copies",
    )(part)


def columns_at(weight_ref, place, cols):
    return weight_ref.at[:, pl.ds(pl.multiple_of(place * cols, LANES), cols)]


def down_kernel(x_ref, hidden_ref, weight_ref, w1, w2, w3, out_ref, own, held, sems, own_sem):
    groups = hidden_ref.shape[0]
    step = held.shape[0] // sems.shape[0]
    place = [lax.rem(x_ref[0] + k, groups) for k in range(groups)]
    fetch = pltpu.make_async_copy(columns_at(weight_ref, x_ref[0], own.shape[1]), own, own_sem)
    fetch.start()
    copies = []

    def dot(left, right):
        return jnp.dot(left, right, preferred_element_type=jnp.float32)

    for i in range(sems.shape[0]):
        rows = pl.ds(i * step, step)
        total = dot(hidden_ref[place[1], rows], w1[...])
        total = total + dot(hidden_ref[place[2], rows], w2[...])
        total = total + dot(hidden_ref[place[3], rows], w3[...])
        if i == 0:
            fetch.wait()
        total = total + dot(hidden_ref[place[0], rows], own[...])
        held[rows] = total.astype(BF)
        copies.append(pltpu.make_async_copy(held.at[rows], out_ref.at[rows], sems.at[i]))
        copies[-1].start()
    for copy in copies:
        copy.wait()


def down_rows(x, hidden, weight, after, far, before):
    own = jax.ShapeDtypeStruct(after.shape, BF)
    out = jax.ShapeDtypeStruct((hidden.shape[1], own.shape[1]), BF)
    return pl.pallas_call(
        down_kernel,
        out_shape=out,
        in_specs=[pl.BlockSpec(memory_space=pltpu.SMEM), INSIDE, OUTSIDE] + [INSIDE] * 3,
        out_specs=OUTSIDE,
        scratch_shapes=[
            pltpu.VMEM(own.shape, BF),
            pltpu.VMEM(out.shape, BF),
            pltpu.SemaphoreType.DMA((2,)),
            pltpu.SemaphoreType.DMA(()),
        ],
        compiler_params=pltpu.CompilerParams(vmem_limit_bytes=VMEM),
        cost_estimate=cost(2 * hidden.size * own.shape[1], hidden, own, own, own, own, out),
        name="down_rows",
    )(x.reshape(1), hidden, weight, after, far, before)


def shift(array, by, tp):
    return lax.ppermute(array, "tp", [(i, (i + by) % tp) for i in range(tp)])


def shards(queries, latent_cache, cache_lengths, moe_tokens, expert_ids, gate_scores, up_weight, down_weight):
    tp = lax.axis_size("tp")
    x = lax.axis_index("tp")
    rows, width = moe_tokens.shape
    cols = width // tp
    group = up_weight.shape[2]
    near = lax.axis_size(NEAR)
    away = lax.axis_size(FAR)
    slots = away * CAP

    up = lax.all_to_all(up_weight[0].reshape(tp, cols, group), "tp", 0, 0, tiled=True)

    mine = lax.dynamic_slice_in_dim(moe_tokens, x * cols, cols, 1)
    packed = jnp.concatenate([mine, routing_columns(expert_ids, gate_scores)], axis=1)
    packed = lax.all_gather(packed, FAR, axis=0, tiled=True)
    packed, up = lax.optimization_barrier((packed, up))
    first = lax.axis_index(FAR) * near
    outgoing = placed_rows(first, packed, rows, near, slots)

    weight = down_weight[0]
    far, before, after = (
        shift(lax.dynamic_slice_in_dim(weight, (x + k) % tp * cols, cols, 1), k, tp) for k in (2, 1, tp - 1)
    )
    received = lax.all_to_all(outgoing.reshape(near, slots, cols), NEAR, 0, 0, tiled=True)
    received, far, before, after = lax.optimization_barrier(
        (received.reshape(near * slots, cols), far, before, after)
    )
    take = shares(packed[:, cols:], rows, first, near, away)

    part = lax.all_to_all(up_parts(received, up), "tp", 0, 0, tiled=True)
    hidden = lax.all_to_all(hidden_copies(part), "tp", 0, 0, tiled=True)
    output = down_rows(x, hidden, weight, after, far, before)

    returned = lax.all_to_all(output.reshape(near, slots, cols), NEAR, 0, 0, tiled=True)

    asked = [queries] + [shift(queries, k, tp) for k in range(1, tp)]
    own = attend_own(asked, latent_cache, cache_lengths, x * latent_cache.shape[1])
    returned, own = lax.optimization_barrier((returned, own))
    shared = [own[0]] + [shift(own[k], tp - k, tp) for k in range(1, tp)]

    mixed = jnp.dot(take, returned.reshape(near * slots, cols), preferred_element_type=jnp.float32)
    mixed = (mixed[: away * rows] + mixed[away * rows :]).astype(BF).reshape(away, rows, cols)
    mixed = lax.all_to_all(mixed, FAR, 0, 0, tiled=True)
    attention_out = merge(shared)
    expert_mix = jnp.sum(mixed.astype(jnp.float32), axis=0).astype(BF)
    return (attention_out, expert_mix)


def solution(mesh):
    devices = mesh.devices
    split = Mesh(devices.reshape(4, 4, 4, 2, devices.shape[1]), EP + ("tp",))
    placed = (
        P(EP, "tp", None),
        P(EP, "tp", None),
        P(EP),
        P(EP, None),
        P(EP, None),
        P(EP, None),
        P(EP, None, "tp"),
        P(EP, "tp", None),
    )
    return jax.shard_map(
        shards,
        mesh=split,
        in_specs=placed,
        out_specs=(P(EP, "tp", None), P(EP, "tp")),
        check_vma=False,
    )
```

```python
import functools

import jax
import jax.numpy as jnp
from jax import lax
from jax.experimental import pallas as pl
from jax.experimental.pallas import tpu as pltpu
from jax.sharding import Mesh, PartitionSpec as P

LATENT = 512
TOP = 8
CAP = 4
SCALE = 192.0 ** (-0.5)
ROUTE_SCALE = 2.5
NEGATIVE = -1e30
LANES = 128
VMEM = 12 << 20
INSIDE = pl.BlockSpec(memory_space=pltpu.VMEM)
OUTSIDE = pl.BlockSpec(memory_space=pltpu.HBM)

EP = ("zh", "zl", "y", "c")
NEAR = ("zl", "y", "c")
FAR = "zh"
BF = jnp.bfloat16


def cost(flops, *arrays):
    size = sum(a.size * a.dtype.itemsize for a in arrays)
    return pl.CostEstimate(flops=flops, bytes_accessed=size, transcendentals=0)


def attend_kernel(place_ref, q0, q1, q2, q3, cache_ref, out_ref):
    r = pl.program_id(0)
    keys = cache_ref[0]
    asked = [q[0] for q in (q0, q1, q2, q3)]
    count = asked[0].shape[0]
    scores = jnp.dot(jnp.concatenate(asked, axis=0), keys, preferred_element_type=jnp.float32) * SCALE
    positions = place_ref[2] + lax.broadcasted_iota(jnp.int32, scores.shape, 1)
    visible = positions < place_ref[r]
    scores = jnp.where(visible, scores, NEGATIVE)
    peak = jnp.max(scores, axis=1, keepdims=True)
    weights = jnp.where(visible, jnp.exp(scores - peak), 0.0)
    total = jnp.sum(weights, axis=1, keepdims=True)
    mixed = lax.dot_general(
        weights.astype(BF), keys[:LATENT], (((1,), (1,)), ((), ())), preferred_element_type=jnp.float32
    )
    mean = (mixed / jnp.where(total > 0.0, total, 1.0)).astype(BF)
    lane = lax.broadcasted_iota(jnp.int32, (scores.shape[0], LANES), 1)
    stats = jnp.zeros((scores.shape[0], LANES), jnp.float32)
    for first, value in ((0, peak), (3, total)):
        for i in range(3):
            part = value.astype(BF).astype(jnp.float32)
            stats = jnp.where(lane == first + i, part, stats)
            value = value - part
    stats = stats.astype(BF)
    for k in range(4):
        out_ref[k, 0, :, :LATENT] = mean[k * count : (k + 1) * count]
        out_ref[k, 0, :, LATENT:] = stats[k * count : (k + 1) * count]


def attend_own(asked, cache, cache_lengths, first):
    keys = jnp.swapaxes(cache, 1, 2)
    count = asked[0].shape[1]
    rows, channels, positions = keys.shape
    out = jax.ShapeDtypeStruct((len(asked), rows, count, LATENT + LANES), BF)
    place = jnp.concatenate([cache_lengths, first.reshape(1).astype(jnp.int32)])
    return pl.pallas_call(
        attend_kernel,
        out_shape=out,
        grid_spec=pltpu.PrefetchScalarGridSpec(
            num_scalar_prefetch=1,
            grid=(rows,),
            in_specs=[pl.BlockSpec((1, count, channels), lambda r, place: (r, 0, 0))] * len(asked)
            + [pl.BlockSpec((1, channels, positions), lambda r, place: (r, 0, 0))],
            out_specs=pl.BlockSpec((len(asked), 1, count, LATENT + LANES), lambda r, place: (0, r, 0, 0)),
        ),
        compiler_params=pltpu.CompilerParams(vmem_limit_bytes=VMEM),
        cost_estimate=cost(4 * rows * 4 * count * channels * positions, cache, out),
        name="attend_own",
    )(place, *asked, keys)


def merge(parts):
    means = [p[..., :LATENT].astype(jnp.float32) for p in parts]
    stats = [p[..., LATENT : LATENT + 6].astype(jnp.float32) for p in parts]
    peaks = [q[..., 0] + q[..., 1] + q[..., 2] for q in stats]
    totals = [q[..., 3] + q[..., 4] + q[..., 5] for q in stats]
    peak = jnp.max(jnp.stack(peaks), axis=0)
    shares = [t * jnp.exp(p - peak) for p, t in zip(peaks, totals)]
    whole = sum(shares)
    return sum((s / whole)[..., None] * m for s, m in zip(shares, means)).astype(BF)


def routing_columns(expert_ids, gate_scores):
    route = gate_scores / jnp.sum(gate_scores, axis=1, keepdims=True) * ROUTE_SCALE
    high = lax.reduce_precision(route, 8, 7)
    low = route - high
    rows = expert_ids.shape[0]
    parts = [expert_ids.astype(BF), high.astype(BF), low.astype(BF)]
    return jnp.concatenate(parts + [jnp.zeros((rows, LANES - 3 * TOP), BF)], axis=1)


def place_kernel(first_ref, packed_ref, out_ref, held, sems, *, rows, experts, slots):
    total, wide = packed_ref.shape
    cols = wide - LANES
    ids = packed_ref[:, cols:].astype(jnp.float32).T
    own = (first_ref[0] + lax.broadcasted_iota(jnp.int32, (experts, total), 0)).astype(jnp.float32)
    named = own == ids[0:1]
    for k in range(1, TOP):
        named = named | (own == ids[k : k + 1])
    before, after = (lax.broadcasted_iota(jnp.int32, (total, total), d) for d in (0, 1))
    earlier = (before < after) & (before // rows == after // rows)
    rank = jnp.dot(
        jnp.where(named, 1.0, 0.0).astype(BF),
        jnp.where(earlier, 1.0, 0.0).astype(BF),
        preferred_element_type=jnp.float32,
    )
    block = lax.broadcasted_iota(jnp.int32, (experts, total), 1) // rows
    slot = jnp.where(named, rank + (block * CAP).astype(jnp.float32), -1.0)
    place = lax.broadcasted_iota(jnp.int32, (experts, slots, total), 1).astype(jnp.float32)
    put = jnp.where(jnp.broadcast_to(slot[:, None, :], place.shape) == place, 1.0, 0.0)
    put = put.reshape(experts * slots, total).astype(BF)
    step = held.shape[0] // sems.shape[0]
    copies = []
    for i in range(sems.shape[0]):
        part = pl.ds(i * step, step)
        moved = jnp.dot(put[i * step : (i + 1) * step], packed_ref[:, :cols], preferred_element_type=jnp.float32)
        held[part] = moved.astype(BF)
        copies.append(pltpu.make_async_copy(held.at[part], out_ref.at[part], sems.at[i]))
        copies[-1].start()
    for copy in copies:
        copy.wait()


def placed_rows(first, packed, rows, experts, slots):
    total, wide = packed.shape
    out = jax.ShapeDtypeStruct((experts * slots, wide - LANES), BF)
    return pl.pallas_call(
        functools.partial(place_kernel, rows=rows, experts=experts, slots=slots),
        out_shape=out,
        in_specs=[pl.BlockSpec(memory_space=pltpu.SMEM), INSIDE],
        out_specs=OUTSIDE,
        scratch_shapes=[pltpu.VMEM(out.shape, BF), pltpu.SemaphoreType.DMA((4,))],
        compiler_params=pltpu.CompilerParams(vmem_limit_bytes=VMEM),
        cost_estimate=cost(2 * out.size * total, packed, out),
        name="placed_rows",
    )(first.reshape(1), packed)


def shares(columns, rows, first, experts, blocks):
    ids = columns[:, :TOP].astype(jnp.float32)
    high = columns[:, TOP : 2 * TOP].astype(jnp.float32)
    low = columns[:, 2 * TOP : 3 * TOP].astype(jnp.float32)
    own = (first + jnp.arange(experts, dtype=jnp.int32)).astype(jnp.float32)
    hit = ids[:, :, None] == own[None, None, :]
    named = jnp.any(hit, axis=1)
    w_high = jnp.sum(jnp.where(hit, high[:, :, None], 0.0), axis=1)
    w_low = jnp.sum(jnp.where(hit, low[:, :, None], 0.0), axis=1)
    total = rows * blocks
    t = jnp.arange(total, dtype=jnp.int32)
    before = (t[None, :] < t[:, None]) & (t[None, :] // rows == t[:, None] // rows)
    rank = jnp.dot(before.astype(BF), named.astype(BF), preferred_element_type=jnp.float32)
    slot = rank + ((t // rows) * CAP).astype(jnp.float32)[:, None]
    slot = jnp.where(named, slot, -1.0)
    slots = jnp.arange(blocks * CAP, dtype=jnp.int32).astype(jnp.float32)
    take = slot[:, :, None] == slots[None, None, :]
    c_high = jnp.where(take, w_high[:, :, None], 0.0).astype(BF).reshape(total, -1)
    c_low = jnp.where(take, w_low[:, :, None], 0.0).astype(BF).reshape(total, -1)
    return jnp.concatenate([c_high, c_low], axis=0)


def up_kernel(rows_ref, weight_ref, out_ref):
    count = rows_ref.shape[0]
    for j in range(weight_ref.shape[0]):
        part = jnp.dot(rows_ref[...], weight_ref[j], preferred_element_type=jnp.float32).astype(BF)
        for i in range(part.shape[1] // LANES):
            out_ref[j, i * count : (i + 1) * count] = part[:, i * LANES : (i + 1) * LANES]


def up_parts(rows, weight):
    groups, depth, width = weight.shape
    count = rows.shape[0]
    out = jax.ShapeDtypeStruct((groups, count * width // LANES, LANES), BF)
    return pl.pallas_call(
        up_kernel,
        out_shape=out,
        in_specs=[INSIDE, INSIDE],
        out_specs=INSIDE,
        compiler_params=pltpu.CompilerParams(vmem_limit_bytes=VMEM),
        cost_estimate=cost(2 * count * depth * width * groups, rows, weight, out),
        name="up_parts",
    )(rows, weight)


def hidden_kernel(part_ref, out_ref):
    groups, count, _ = part_ref.shape
    step = count // 4
    for i in range(4):
        rows = pl.ds(i * step, step)
        value = part_ref[0, rows].astype(jnp.float32)
        for j in range(1, groups):
            value = value + part_ref[j, rows].astype(jnp.float32)
        value = (value / (1.0 + jnp.exp(-value))).astype(BF)
        for j in range(groups):
            out_ref[j, rows] = value


def hidden_copies(part):
    return pl.pallas_call(
        hidden_kernel,
        out_shape=jax.ShapeDtypeStruct(part.shape, BF),
        in_specs=[INSIDE],
        out_specs=INSIDE,
        compiler_params=pltpu.CompilerParams(vmem_limit_bytes=VMEM),
        cost_estimate=cost(10 * part.size, part, part),
        name="hidden_copies",
    )(part)


def columns_at(weight_ref, place, cols):
    return weight_ref.at[:, pl.ds(pl.multiple_of(place * cols, LANES), cols)]


def down_kernel(x_ref, hidden_ref, weight_ref, w1, w2, w3, out_ref, own, held, sems, own_sem):
    groups, count = hidden_ref.shape[0], held.shape[0]
    step = held.shape[0] // sems.shape[0]
    place = [lax.rem(x_ref[0] + k, groups) for k in range(groups)]
    fetch = pltpu.make_async_copy(columns_at(weight_ref, x_ref[0], own.shape[1]), own, own_sem)
    fetch.start()
    copies = []

    def dot(left, right):
        return jnp.dot(left, right, preferred_element_type=jnp.float32)

    def group(j, i):
        halves = [hidden_ref[j, pl.ds(h * count + i * step, step)] for h in range(hidden_ref.shape[1] // count)]
        return jnp.concatenate(halves, axis=1)

    for i in range(sems.shape[0]):
        rows = pl.ds(i * step, step)
        total = dot(group(place[1], i), w1[...])
        total = total + dot(group(place[2], i), w2[...])
        total = total + dot(group(place[3], i), w3[...])
        if i == 0:
            fetch.wait()
        total = total + dot(group(place[0], i), own[...])
        held[rows] = total.astype(BF)
        copies.append(pltpu.make_async_copy(held.at[rows], out_ref.at[rows], sems.at[i]))
        copies[-1].start()
    for copy in copies:
        copy.wait()


def down_rows(x, hidden, weight, after, far, before):
    own = jax.ShapeDtypeStruct(after.shape, BF)
    out = jax.ShapeDtypeStruct((hidden.shape[1] * LANES // own.shape[0], own.shape[1]), BF)
    return pl.pallas_call(
        down_kernel,
        out_shape=out,
        in_specs=[pl.BlockSpec(memory_space=pltpu.SMEM), INSIDE, OUTSIDE] + [INSIDE] * 3,
        out_specs=OUTSIDE,
        scratch_shapes=[
            pltpu.VMEM(own.shape, BF),
            pltpu.VMEM(out.shape, BF),
            pltpu.SemaphoreType.DMA((2,)),
            pltpu.SemaphoreType.DMA(()),
        ],
        compiler_params=pltpu.CompilerParams(vmem_limit_bytes=VMEM),
        cost_estimate=cost(2 * hidden.size * own.shape[1], hidden, own, own, own, own, out),
        name="down_rows",
    )(x.reshape(1), hidden, weight, after, far, before)


def mix_kernel(take_ref, rows_ref, out_ref, held, sem):
    groups, lines, _ = held.shape
    total = take_ref.shape[0] // 2
    count = total // groups
    mixed = jnp.dot(take_ref[...], rows_ref[...], preferred_element_type=jnp.float32)
    mixed = (mixed[:total] + mixed[total:]).astype(BF)
    for j in range(groups):
        for i in range(lines // count):
            part = mixed[j * count : (j + 1) * count, i * LANES : (i + 1) * LANES]
            held[j, i * count : (i + 1) * count] = part
    copy = pltpu.make_async_copy(held, out_ref, sem)
    copy.start()
    copy.wait()


def mixed_rows(take, rows, groups):
    total, cols = take.shape[0] // 2, rows.shape[1]
    out = jax.ShapeDtypeStruct((groups, total // groups * cols // LANES, LANES), BF)
    return pl.pallas_call(
        mix_kernel,
        out_shape=out,
        in_specs=[INSIDE, INSIDE],
        out_specs=OUTSIDE,
        scratch_shapes=[pltpu.VMEM(out.shape, BF), pltpu.SemaphoreType.DMA(())],
        compiler_params=pltpu.CompilerParams(vmem_limit_bytes=VMEM),
        cost_estimate=cost(2 * take.size * cols, take, rows, out),
        name="mixed_rows",
    )(take, rows)


def sum_kernel(parts_ref, out_ref):
    count = out_ref.shape[0]
    for i in range(out_ref.shape[1] // LANES):
        rows = pl.ds(i * count, count)
        total = parts_ref[0, rows].astype(jnp.float32)
        for j in range(1, parts_ref.shape[0]):
            total = total + parts_ref[j, rows].astype(jnp.float32)
        out_ref[:, i * LANES : (i + 1) * LANES] = total.astype(BF)


def summed(parts, rows, cols):
    out = jax.ShapeDtypeStruct((rows, cols), BF)
    return pl.pallas_call(
        sum_kernel,
        out_shape=out,
        in_specs=[INSIDE],
        out_specs=INSIDE,
        compiler_params=pltpu.CompilerParams(vmem_limit_bytes=VMEM),
        cost_estimate=cost(parts.size, parts, out),
        name="summed",
    )(parts)


def shift(array, by, tp):
    return lax.ppermute(array, "tp", [(i, (i + by) % tp) for i in range(tp)])


def shards(queries, latent_cache, cache_lengths, moe_tokens, expert_ids, gate_scores, up_weight, down_weight):
    tp = lax.axis_size("tp")
    x = lax.axis_index("tp")
    rows, width = moe_tokens.shape
    cols = width // tp
    group = up_weight.shape[2]
    near = lax.axis_size(NEAR)
    away = lax.axis_size(FAR)
    slots = away * CAP

    up = lax.all_to_all(up_weight[0].reshape(tp, cols, group), "tp", 0, 0, tiled=True)

    mine = lax.dynamic_slice_in_dim(moe_tokens, x * cols, cols, 1)
    packed = jnp.concatenate([mine, routing_columns(expert_ids, gate_scores)], axis=1)
    packed = lax.all_gather(packed, FAR, axis=0, tiled=True)
    first = lax.axis_index(FAR) * near
    outgoing = placed_rows(first, packed, rows, near, slots)

    weight = down_weight[0]
    cut = [lax.dynamic_slice_in_dim(weight, (x + k) % tp * cols, cols, 1) for k in (2, 1, tp - 1)]
    outgoing, up, cut = lax.optimization_barrier((outgoing, up, cut))
    far, before, after = (shift(block, k, tp) for block, k in zip(cut, (2, 1, tp - 1)))
    received = lax.all_to_all(outgoing.reshape(near, slots, cols), NEAR, 0, 0, tiled=True)
    received, far, before, after = lax.optimization_barrier(
        (received.reshape(near * slots, cols), far, before, after)
    )
    take = shares(packed[:, cols:], rows, first, near, away)

    part = lax.all_to_all(up_parts(received, up), "tp", 0, 0, tiled=True)
    hidden = lax.all_to_all(hidden_copies(part), "tp", 0, 0, tiled=True)
    output = down_rows(x, hidden, weight, after, far, before)

    returned = lax.all_to_all(output.reshape(near, slots, cols), NEAR, 0, 0, tiled=True)

    asked = [queries] + [shift(queries, k, tp) for k in range(1, tp)]
    own = attend_own(asked, latent_cache, cache_lengths, x * latent_cache.shape[1])
    returned, own = lax.optimization_barrier((returned, own))
    shared = [own[0]] + [shift(own[k], tp - k, tp) for k in range(1, tp)]

    mixed = mixed_rows(take, returned.reshape(near * slots, cols), away)
    mixed = lax.all_to_all(mixed, FAR, 0, 0, tiled=True)
    attention_out = merge(shared)
    expert_mix = summed(mixed, rows, cols)
    return (attention_out, expert_mix)


def solution(mesh):
    devices = mesh.devices
    split = Mesh(devices.reshape(4, 4, 4, 2, devices.shape[1]), EP + ("tp",))
    placed = (
        P(EP, "tp", None),
        P(EP, "tp", None),
        P(EP),
        P(EP, None),
        P(EP, None),
        P(EP, None),
        P(EP, None, "tp"),
        P(EP, "tp", None),
    )
    return jax.shard_map(
        shards,
        mesh=split,
        in_specs=placed,
        out_specs=(P(EP, "tp", None), P(EP, "tp")),
        check_vma=False,
    )
```

```python
import functools

import jax
import jax.numpy as jnp
from jax import lax
from jax.experimental import pallas as pl
from jax.experimental.pallas import tpu as pltpu
from jax.sharding import Mesh, PartitionSpec as P

LATENT = 512
TOP = 8
CAP = 4
SCALE = 192.0 ** (-0.5)
ROUTE_SCALE = 2.5
NEGATIVE = -1e30
LANES = 128
VMEM = 12 << 20
INSIDE = pl.BlockSpec(memory_space=pltpu.VMEM)
OUTSIDE = pl.BlockSpec(memory_space=pltpu.HBM)

EP = ("zh", "zl", "y", "c")
NEAR = ("zl", "y", "c")
FAR = "zh"
BF = jnp.bfloat16


def cost(flops, *arrays):
    size = sum(a.size * a.dtype.itemsize for a in arrays)
    return pl.CostEstimate(flops=flops, bytes_accessed=size, transcendentals=0)


def attend_kernel(place_ref, q0, q1, q2, q3, cache_ref, out_ref):
    r = pl.program_id(0)
    keys = cache_ref[0]
    asked = [q[0] for q in (q0, q1, q2, q3)]
    count = asked[0].shape[0]
    scores = jnp.dot(jnp.concatenate(asked, axis=0), keys, preferred_element_type=jnp.float32) * SCALE
    positions = place_ref[2] + lax.broadcasted_iota(jnp.int32, scores.shape, 1)
    visible = positions < place_ref[r]
    scores = jnp.where(visible, scores, NEGATIVE)
    peak = jnp.max(scores, axis=1, keepdims=True)
    weights = jnp.where(visible, jnp.exp(scores - peak), 0.0)
    total = jnp.sum(weights, axis=1, keepdims=True)
    mixed = lax.dot_general(
        weights.astype(BF), keys[:LATENT], (((1,), (1,)), ((), ())), preferred_element_type=jnp.float32
    )
    mean = (mixed / jnp.where(total > 0.0, total, 1.0)).astype(BF)
    lane = lax.broadcasted_iota(jnp.int32, (scores.shape[0], LANES), 1)
    stats = jnp.zeros((scores.shape[0], LANES), jnp.float32)
    for first, value in ((0, peak), (3, total)):
        for i in range(3):
            part = value.astype(BF).astype(jnp.float32)
            stats = jnp.where(lane == first + i, part, stats)
            value = value - part
    stats = stats.astype(BF)
    for k in range(4):
        out_ref[k, 0, :, :LATENT] = mean[k * count : (k + 1) * count]
        out_ref[k, 0, :, LATENT:] = stats[k * count : (k + 1) * count]


def attend_own(asked, cache, cache_lengths, first):
    keys = jnp.swapaxes(cache, 1, 2)
    count = asked[0].shape[1]
    rows, channels, positions = keys.shape
    out = jax.ShapeDtypeStruct((len(asked), rows, count, LATENT + LANES), BF)
    place = jnp.concatenate([cache_lengths, first.reshape(1).astype(jnp.int32)])
    return pl.pallas_call(
        attend_kernel,
        out_shape=out,
        grid_spec=pltpu.PrefetchScalarGridSpec(
            num_scalar_prefetch=1,
            grid=(rows,),
            in_specs=[pl.BlockSpec((1, count, channels), lambda r, place: (r, 0, 0))] * len(asked)
            + [pl.BlockSpec((1, channels, positions), lambda r, place: (r, 0, 0))],
            out_specs=pl.BlockSpec((len(asked), 1, count, LATENT + LANES), lambda r, place: (0, r, 0, 0)),
        ),
        compiler_params=pltpu.CompilerParams(vmem_limit_bytes=VMEM),
        cost_estimate=cost(4 * rows * 4 * count * channels * positions, cache, out),
        name="attend_own",
    )(place, *asked, keys)


def merge(parts):
    means = [p[..., :LATENT].astype(jnp.float32) for p in parts]
    stats = [p[..., LATENT : LATENT + 6].astype(jnp.float32) for p in parts]
    peaks = [q[..., 0] + q[..., 1] + q[..., 2] for q in stats]
    totals = [q[..., 3] + q[..., 4] + q[..., 5] for q in stats]
    peak = jnp.max(jnp.stack(peaks), axis=0)
    shares = [t * jnp.exp(p - peak) for p, t in zip(peaks, totals)]
    whole = sum(shares)
    return sum((s / whole)[..., None] * m for s, m in zip(shares, means)).astype(BF)


def routing_columns(expert_ids, gate_scores):
    route = gate_scores / jnp.sum(gate_scores, axis=1, keepdims=True) * ROUTE_SCALE
    high = lax.reduce_precision(route, 8, 7)
    low = route - high
    rows = expert_ids.shape[0]
    parts = [expert_ids.astype(BF), high.astype(BF), low.astype(BF)]
    return jnp.concatenate(parts + [jnp.zeros((rows, LANES - 3 * TOP), BF)], axis=1)


def place_kernel(first_ref, packed_ref, out_ref, held, sems, *, rows, experts, slots):
    total, wide = packed_ref.shape
    cols = wide - LANES
    ids = packed_ref[:, cols:].astype(jnp.float32).T
    own = (first_ref[0] + lax.broadcasted_iota(jnp.int32, (experts, total), 0)).astype(jnp.float32)
    named = own == ids[0:1]
    for k in range(1, TOP):
        named = named | (own == ids[k : k + 1])
    before, after = (lax.broadcasted_iota(jnp.int32, (total, total), d) for d in (0, 1))
    earlier = (before < after) & (before // rows == after // rows)
    rank = jnp.dot(
        jnp.where(named, 1.0, 0.0).astype(BF),
        jnp.where(earlier, 1.0, 0.0).astype(BF),
        preferred_element_type=jnp.float32,
    )
    block = lax.broadcasted_iota(jnp.int32, (experts, total), 1) // rows
    slot = jnp.where(named, rank + (block * CAP).astype(jnp.float32), -1.0)
    place = lax.broadcasted_iota(jnp.int32, (experts, slots, total), 1).astype(jnp.float32)
    put = jnp.where(jnp.broadcast_to(slot[:, None, :], place.shape) == place, 1.0, 0.0)
    put = put.reshape(experts * slots, total).astype(BF)
    step = held.shape[0] // sems.shape[0]
    copies = []
    for i in range(sems.shape[0]):
        part = pl.ds(i * step, step)
        moved = jnp.dot(put[i * step : (i + 1) * step], packed_ref[:, :cols], preferred_element_type=jnp.float32)
        held[part] = moved.astype(BF)
        copies.append(pltpu.make_async_copy(held.at[part], out_ref.at[part], sems.at[i]))
        copies[-1].start()
    for copy in copies:
        copy.wait()


def placed_rows(first, packed, rows, experts, slots):
    total, wide = packed.shape
    out = jax.ShapeDtypeStruct((experts * slots, wide - LANES), BF)
    return pl.pallas_call(
        functools.partial(place_kernel, rows=rows, experts=experts, slots=slots),
        out_shape=out,
        in_specs=[pl.BlockSpec(memory_space=pltpu.SMEM), INSIDE],
        out_specs=OUTSIDE,
        scratch_shapes=[pltpu.VMEM(out.shape, BF), pltpu.SemaphoreType.DMA((4,))],
        compiler_params=pltpu.CompilerParams(vmem_limit_bytes=VMEM),
        cost_estimate=cost(2 * out.size * total, packed, out),
        name="placed_rows",
    )(first.reshape(1), packed)


def shares(columns, rows, first, experts, blocks):
    ids = columns[:, :TOP].astype(jnp.float32)
    high = columns[:, TOP : 2 * TOP].astype(jnp.float32)
    low = columns[:, 2 * TOP : 3 * TOP].astype(jnp.float32)
    own = (first + jnp.arange(experts, dtype=jnp.int32)).astype(jnp.float32)
    hit = ids[:, :, None] == own[None, None, :]
    named = jnp.any(hit, axis=1)
    w_high = jnp.sum(jnp.where(hit, high[:, :, None], 0.0), axis=1)
    w_low = jnp.sum(jnp.where(hit, low[:, :, None], 0.0), axis=1)
    total = rows * blocks
    t = jnp.arange(total, dtype=jnp.int32)
    before = (t[None, :] < t[:, None]) & (t[None, :] // rows == t[:, None] // rows)
    rank = jnp.dot(before.astype(BF), named.astype(BF), preferred_element_type=jnp.float32)
    slot = rank + ((t // rows) * CAP).astype(jnp.float32)[:, None]
    slot = jnp.where(named, slot, -1.0)
    slots = jnp.arange(blocks * CAP, dtype=jnp.int32).astype(jnp.float32)
    take = slot[:, :, None] == slots[None, None, :]
    c_high = jnp.where(take, w_high[:, :, None], 0.0).astype(BF).reshape(total, -1)
    c_low = jnp.where(take, w_low[:, :, None], 0.0).astype(BF).reshape(total, -1)
    return jnp.concatenate([c_high, c_low], axis=0)


def up_kernel(rows_ref, weight_ref, out_ref):
    count = rows_ref.shape[0]
    for j in range(weight_ref.shape[0]):
        part = jnp.dot(rows_ref[...], weight_ref[j], preferred_element_type=jnp.float32).astype(BF)
        for i in range(part.shape[1] // LANES):
            out_ref[j, i * count : (i + 1) * count] = part[:, i * LANES : (i + 1) * LANES]


def up_parts(rows, weight):
    groups, depth, width = weight.shape
    count = rows.shape[0]
    out = jax.ShapeDtypeStruct((groups, count * width // LANES, LANES), BF)
    return pl.pallas_call(
        up_kernel,
        out_shape=out,
        in_specs=[INSIDE, INSIDE],
        out_specs=INSIDE,
        compiler_params=pltpu.CompilerParams(vmem_limit_bytes=VMEM),
        cost_estimate=cost(2 * count * depth * width * groups, rows, weight, out),
        name="up_parts",
    )(rows, weight)


def hidden_kernel(part_ref, out_ref):
    groups, count, _ = part_ref.shape
    step = count // 4
    for i in range(4):
        rows = pl.ds(i * step, step)
        value = part_ref[0, rows].astype(jnp.float32)
        for j in range(1, groups):
            value = value + part_ref[j, rows].astype(jnp.float32)
        value = (value / (1.0 + jnp.exp(-value))).astype(BF)
        for j in range(groups):
            out_ref[j, rows] = value


def hidden_copies(part):
    return pl.pallas_call(
        hidden_kernel,
        out_shape=jax.ShapeDtypeStruct(part.shape, BF),
        in_specs=[INSIDE],
        out_specs=INSIDE,
        compiler_params=pltpu.CompilerParams(vmem_limit_bytes=VMEM),
        cost_estimate=cost(10 * part.size, part, part),
        name="hidden_copies",
    )(part)


def columns_at(weight_ref, place, cols):
    return weight_ref.at[:, pl.ds(pl.multiple_of(place * cols, LANES), cols)]


def down_kernel(x_ref, hidden_ref, weight_ref, w1, w2, w3, out_ref, near, held, near_sems, sems):
    groups, count = hidden_ref.shape[0], held.shape[0]
    step = count // sems.shape[0]
    place = [lax.rem(x_ref[0] + k, groups) for k in range(groups)]
    sources = [columns_at(weight_ref, x_ref[0], near.shape[2]), w1, w2, w3]
    fetches = [pltpu.make_async_copy(source, near.at[k], near_sems.at[k]) for k, source in enumerate(sources)]
    for fetch in fetches:
        fetch.start()
    copies = []

    def part(k, i):
        parts = hidden_ref.shape[1] // count
        lines = [hidden_ref[place[k], pl.ds(h * count + i * step, step)] for h in range(parts)]
        return jnp.dot(jnp.concatenate(lines, axis=1), near[k], preferred_element_type=jnp.float32)

    for i in range(sems.shape[0]):
        rows = pl.ds(i * step, step)
        total = None
        for k in range(groups):
            if i == 0:
                fetches[k].wait()
            total = part(k, i) if k == 0 else total + part(k, i)
        held[rows] = total.astype(BF)
        copies.append(pltpu.make_async_copy(held.at[rows], out_ref.at[rows], sems.at[i]))
        copies[-1].start()
    for copy in copies:
        copy.wait()


def down_rows(x, hidden, weight, after, far, before):
    width, cols = after.shape
    groups, lines, _ = hidden.shape
    out = jax.ShapeDtypeStruct((lines * LANES // width, cols), BF)
    return pl.pallas_call(
        down_kernel,
        out_shape=out,
        in_specs=[pl.BlockSpec(memory_space=pltpu.SMEM), INSIDE] + [OUTSIDE] * 4,
        out_specs=OUTSIDE,
        scratch_shapes=[
            pltpu.VMEM((groups, width, cols), BF),
            pltpu.VMEM(out.shape, BF),
            pltpu.SemaphoreType.DMA((groups,)),
            pltpu.SemaphoreType.DMA((2,)),
        ],
        compiler_params=pltpu.CompilerParams(vmem_limit_bytes=VMEM),
        cost_estimate=cost(2 * hidden.size * cols, hidden, after, after, after, after, out),
        name="down_rows",
    )(x.reshape(1), hidden, weight, after, far, before)


def mix_kernel(take_ref, rows_ref, out_ref, held, sem):
    groups, lines, _ = held.shape
    total = take_ref.shape[0] // 2
    count = total // groups
    mixed = jnp.dot(take_ref[...], rows_ref[...], preferred_element_type=jnp.float32)
    mixed = (mixed[:total] + mixed[total:]).astype(BF)
    for j in range(groups):
        for i in range(lines // count):
            part = mixed[j * count : (j + 1) * count, i * LANES : (i + 1) * LANES]
            held[j, i * count : (i + 1) * count] = part
    copy = pltpu.make_async_copy(held, out_ref, sem)
    copy.start()
    copy.wait()


def mixed_rows(take, rows, groups):
    total, cols = take.shape[0] // 2, rows.shape[1]
    out = jax.ShapeDtypeStruct((groups, total // groups * cols // LANES, LANES), BF)
    return pl.pallas_call(
        mix_kernel,
        out_shape=out,
        in_specs=[INSIDE, INSIDE],
        out_specs=OUTSIDE,
        scratch_shapes=[pltpu.VMEM(out.shape, BF), pltpu.SemaphoreType.DMA(())],
        compiler_params=pltpu.CompilerParams(vmem_limit_bytes=VMEM),
        cost_estimate=cost(2 * take.size * cols, take, rows, out),
        name="mixed_rows",
    )(take, rows)


def sum_kernel(parts_ref, out_ref):
    count = out_ref.shape[0]
    for i in range(out_ref.shape[1] // LANES):
        rows = pl.ds(i * count, count)
        total = parts_ref[0, rows].astype(jnp.float32)
        for j in range(1, parts_ref.shape[0]):
            total = total + parts_ref[j, rows].astype(jnp.float32)
        out_ref[:, i * LANES : (i + 1) * LANES] = total.astype(BF)


def summed(parts, rows, cols):
    out = jax.ShapeDtypeStruct((rows, cols), BF)
    return pl.pallas_call(
        sum_kernel,
        out_shape=out,
        in_specs=[INSIDE],
        out_specs=INSIDE,
        compiler_params=pltpu.CompilerParams(vmem_limit_bytes=VMEM),
        cost_estimate=cost(parts.size, parts, out),
        name="summed",
    )(parts)


def shift(array, by, tp):
    return lax.ppermute(array, "tp", [(i, (i + by) % tp) for i in range(tp)])


def shards(queries, latent_cache, cache_lengths, moe_tokens, expert_ids, gate_scores, up_weight, down_weight):
    tp = lax.axis_size("tp")
    x = lax.axis_index("tp")
    rows, width = moe_tokens.shape
    cols = width // tp
    group = up_weight.shape[2]
    near = lax.axis_size(NEAR)
    away = lax.axis_size(FAR)
    slots = away * CAP

    up = lax.all_to_all(up_weight[0].reshape(tp, cols, group), "tp", 0, 0, tiled=True)

    mine = lax.dynamic_slice_in_dim(moe_tokens, x * cols, cols, 1)
    packed = jnp.concatenate([mine, routing_columns(expert_ids, gate_scores)], axis=1)
    packed = lax.all_gather(packed, FAR, axis=0, tiled=True)
    first = lax.axis_index(FAR) * near
    outgoing = placed_rows(first, packed, rows, near, slots)

    weight = down_weight[0]
    cut = [lax.dynamic_slice_in_dim(weight, (x + k) % tp * cols, cols, 1) for k in (2, 1, tp - 1)]
    outgoing, up, cut = lax.optimization_barrier((outgoing, up, cut))
    far, before, after = (shift(block, k, tp) for block, k in zip(cut, (2, 1, tp - 1)))
    received = lax.all_to_all(outgoing.reshape(near, slots, cols), NEAR, 0, 0, tiled=True)
    received = received.reshape(near * slots, cols)
    take = shares(packed[:, cols:], rows, first, near, away)

    part = up_parts(received, up)
    part, far, after, before = lax.optimization_barrier((part, far, after, before))
    part = lax.all_to_all(part, "tp", 0, 0, tiled=True)
    hidden = lax.all_to_all(hidden_copies(part), "tp", 0, 0, tiled=True)
    output = down_rows(x, hidden, weight, after, far, before)

    returned = lax.all_to_all(output.reshape(near, slots, cols), NEAR, 0, 0, tiled=True)

    asked = [queries] + [shift(queries, k, tp) for k in range(1, tp)]
    own = attend_own(asked, latent_cache, cache_lengths, x * latent_cache.shape[1])
    returned, own = lax.optimization_barrier((returned, own))
    shared = [own[0]] + [shift(own[k], tp - k, tp) for k in range(1, tp)]

    mixed = mixed_rows(take, returned.reshape(near * slots, cols), away)
    mixed = lax.all_to_all(mixed, FAR, 0, 0, tiled=True)
    attention_out = merge(shared)
    expert_mix = summed(mixed, rows, cols)
    return (attention_out, expert_mix)


def solution(mesh):
    devices = mesh.devices
    split = Mesh(devices.reshape(4, 4, 4, 2, devices.shape[1]), EP + ("tp",))
    placed = (
        P(EP, "tp", None),
        P(EP, "tp", None),
        P(EP),
        P(EP, None),
        P(EP, None),
        P(EP, None),
        P(EP, None, "tp"),
        P(EP, "tp", None),
    )
    return jax.shard_map(
        shards,
        mesh=split,
        in_specs=placed,
        out_specs=(P(EP, "tp", None), P(EP, "tp")),
        check_vma=False,
    )
```

```python
import functools

import jax
import jax.numpy as jnp
from jax import lax
from jax.experimental import pallas as pl
from jax.experimental.pallas import tpu as pltpu
from jax.sharding import Mesh, PartitionSpec as P

LATENT = 512
TOP = 8
CAP = 4
SCALE = 192.0 ** (-0.5)
ROUTE_SCALE = 2.5
NEGATIVE = -1e30
LANES = 128
VMEM = 12 << 20
INSIDE = pl.BlockSpec(memory_space=pltpu.VMEM)
OUTSIDE = pl.BlockSpec(memory_space=pltpu.HBM)

EP = ("zh", "zl", "y", "c")
NEAR = ("y", "c", "zl")
PLANES, PLANE = 4, 8
FAR = "zh"
BF = jnp.bfloat16


def cost(flops, *arrays):
    size = sum(a.size * a.dtype.itemsize for a in arrays)
    return pl.CostEstimate(flops=flops, bytes_accessed=size, transcendentals=0)


def attend_kernel(place_ref, q0, q1, q2, q3, cache_ref, out_ref):
    r = pl.program_id(0)
    keys = cache_ref[0]
    asked = [q[0] for q in (q0, q1, q2, q3)]
    count = asked[0].shape[0]
    scores = jnp.dot(jnp.concatenate(asked, axis=0), keys, preferred_element_type=jnp.float32) * SCALE
    positions = place_ref[2] + lax.broadcasted_iota(jnp.int32, scores.shape, 1)
    visible = positions < place_ref[r]
    scores = jnp.where(visible, scores, NEGATIVE)
    peak = jnp.max(scores, axis=1, keepdims=True)
    weights = jnp.where(visible, jnp.exp(scores - peak), 0.0)
    total = jnp.sum(weights, axis=1, keepdims=True)
    mixed = lax.dot_general(
        weights.astype(BF), keys[:LATENT], (((1,), (1,)), ((), ())), preferred_element_type=jnp.float32
    )
    mean = (mixed / jnp.where(total > 0.0, total, 1.0)).astype(BF)
    lane = lax.broadcasted_iota(jnp.int32, (scores.shape[0], LANES), 1)
    stats = jnp.zeros((scores.shape[0], LANES), jnp.float32)
    for first, value in ((0, peak), (3, total)):
        for i in range(3):
            part = value.astype(BF).astype(jnp.float32)
            stats = jnp.where(lane == first + i, part, stats)
            value = value - part
    stats = stats.astype(BF)
    for k in range(4):
        out_ref[k, 0, :, :LATENT] = mean[k * count : (k + 1) * count]
        out_ref[k, 0, :, LATENT:] = stats[k * count : (k + 1) * count]


def attend_own(asked, cache, cache_lengths, first):
    keys = jnp.swapaxes(cache, 1, 2)
    count = asked[0].shape[1]
    rows, channels, positions = keys.shape
    out = jax.ShapeDtypeStruct((len(asked), rows, count, LATENT + LANES), BF)
    place = jnp.concatenate([cache_lengths, first.reshape(1).astype(jnp.int32)])
    return pl.pallas_call(
        attend_kernel,
        out_shape=out,
        grid_spec=pltpu.PrefetchScalarGridSpec(
            num_scalar_prefetch=1,
            grid=(rows,),
            in_specs=[pl.BlockSpec((1, count, channels), lambda r, place: (r, 0, 0))] * len(asked)
            + [pl.BlockSpec((1, channels, positions), lambda r, place: (r, 0, 0))],
            out_specs=pl.BlockSpec((len(asked), 1, count, LATENT + LANES), lambda r, place: (0, r, 0, 0)),
        ),
        compiler_params=pltpu.CompilerParams(vmem_limit_bytes=VMEM),
        cost_estimate=cost(4 * rows * 4 * count * channels * positions, cache, out),
        name="attend_own",
    )(place, *asked, keys)


def merge(parts):
    means = [p[..., :LATENT].astype(jnp.float32) for p in parts]
    stats = [p[..., LATENT : LATENT + 6].astype(jnp.float32) for p in parts]
    peaks = [q[..., 0] + q[..., 1] + q[..., 2] for q in stats]
    totals = [q[..., 3] + q[..., 4] + q[..., 5] for q in stats]
    peak = jnp.max(jnp.stack(peaks), axis=0)
    shares = [t * jnp.exp(p - peak) for p, t in zip(peaks, totals)]
    whole = sum(shares)
    return sum((s / whole)[..., None] * m for s, m in zip(shares, means)).astype(BF)


def routing_columns(expert_ids, gate_scores):
    route = gate_scores / jnp.sum(gate_scores, axis=1, keepdims=True) * ROUTE_SCALE
    high = lax.reduce_precision(route, 8, 7)
    low = route - high
    rows = expert_ids.shape[0]
    parts = [expert_ids.astype(BF), high.astype(BF), low.astype(BF)]
    return jnp.concatenate(parts + [jnp.zeros((rows, LANES - 3 * TOP), BF)], axis=1)


def expert_at(first, place):
    return (first + place % PLANES * PLANE + place // PLANES).astype(jnp.float32)


def place_kernel(first_ref, packed_ref, out_ref, held, sems, *, rows, experts, slots):
    total, wide = packed_ref.shape
    cols = wide - LANES
    ids = packed_ref[:, cols:].astype(jnp.float32).T
    own = expert_at(first_ref[0], lax.broadcasted_iota(jnp.int32, (experts, total), 0))
    named = own == ids[0:1]
    for k in range(1, TOP):
        named = named | (own == ids[k : k + 1])
    before, after = (lax.broadcasted_iota(jnp.int32, (total, total), d) for d in (0, 1))
    earlier = (before < after) & (before // rows == after // rows)
    rank = jnp.dot(
        jnp.where(named, 1.0, 0.0).astype(BF),
        jnp.where(earlier, 1.0, 0.0).astype(BF),
        preferred_element_type=jnp.float32,
    )
    block = lax.broadcasted_iota(jnp.int32, (experts, total), 1) // rows
    slot = jnp.where(named, rank + (block * CAP).astype(jnp.float32), -1.0)
    place = lax.broadcasted_iota(jnp.int32, (experts, slots, total), 1).astype(jnp.float32)
    put = jnp.where(jnp.broadcast_to(slot[:, None, :], place.shape) == place, 1.0, 0.0)
    put = put.reshape(experts * slots, total).astype(BF)
    step = held.shape[0] // sems.shape[0]
    copies = []
    for i in range(sems.shape[0]):
        part = pl.ds(i * step, step)
        moved = jnp.dot(put[i * step : (i + 1) * step], packed_ref[:, :cols], preferred_element_type=jnp.float32)
        held[part] = moved.astype(BF)
        copies.append(pltpu.make_async_copy(held.at[part], out_ref.at[part], sems.at[i]))
        copies[-1].start()
    for copy in copies:
        copy.wait()


def placed_rows(first, packed, rows, experts, slots):
    total, wide = packed.shape
    out = jax.ShapeDtypeStruct((experts * slots, wide - LANES), BF)
    return pl.pallas_call(
        functools.partial(place_kernel, rows=rows, experts=experts, slots=slots),
        out_shape=out,
        in_specs=[pl.BlockSpec(memory_space=pltpu.SMEM), INSIDE],
        out_specs=OUTSIDE,
        scratch_shapes=[pltpu.VMEM(out.shape, BF), pltpu.SemaphoreType.DMA((4,))],
        compiler_params=pltpu.CompilerParams(vmem_limit_bytes=VMEM),
        cost_estimate=cost(2 * out.size * total, packed, out),
        name="placed_rows",
    )(first.reshape(1), packed)


def shares(columns, rows, first, experts, blocks):
    ids = columns[:, :TOP].astype(jnp.float32)
    high = columns[:, TOP : 2 * TOP].astype(jnp.float32)
    low = columns[:, 2 * TOP : 3 * TOP].astype(jnp.float32)
    own = expert_at(first, jnp.arange(experts, dtype=jnp.int32))
    hit = ids[:, :, None] == own[None, None, :]
    named = jnp.any(hit, axis=1)
    w_high = jnp.sum(jnp.where(hit, high[:, :, None], 0.0), axis=1)
    w_low = jnp.sum(jnp.where(hit, low[:, :, None], 0.0), axis=1)
    total = rows * blocks
    t = jnp.arange(total, dtype=jnp.int32)
    before = (t[None, :] < t[:, None]) & (t[None, :] // rows == t[:, None] // rows)
    rank = jnp.dot(before.astype(BF), named.astype(BF), preferred_element_type=jnp.float32)
    slot = rank + ((t // rows) * CAP).astype(jnp.float32)[:, None]
    slot = jnp.where(named, slot, -1.0)
    slots = jnp.arange(blocks * CAP, dtype=jnp.int32).astype(jnp.float32)
    take = slot[:, :, None] == slots[None, None, :]
    c_high = jnp.where(take, w_high[:, :, None], 0.0).astype(BF).reshape(total, -1)
    c_low = jnp.where(take, w_low[:, :, None], 0.0).astype(BF).reshape(total, -1)
    return jnp.concatenate([c_high, c_low], axis=0)


def up_kernel(rows_ref, weight_ref, out_ref):
    count = rows_ref.shape[0]
    for j in range(weight_ref.shape[0]):
        part = jnp.dot(rows_ref[...], weight_ref[j], preferred_element_type=jnp.float32).astype(BF)
        for i in range(part.shape[1] // LANES):
            out_ref[j, i * count : (i + 1) * count] = part[:, i * LANES : (i + 1) * LANES]


def up_parts(rows, weight):
    groups, depth, width = weight.shape
    count = rows.shape[0]
    out = jax.ShapeDtypeStruct((groups, count * width // LANES, LANES), BF)
    return pl.pallas_call(
        up_kernel,
        out_shape=out,
        in_specs=[INSIDE, INSIDE],
        out_specs=INSIDE,
        compiler_params=pltpu.CompilerParams(vmem_limit_bytes=VMEM),
        cost_estimate=cost(2 * count * depth * width * groups, rows, weight, out),
        name="up_parts",
    )(rows, weight)


def hidden_kernel(part_ref, out_ref):
    groups, count, _ = part_ref.shape
    step = count // 4
    for i in range(4):
        rows = pl.ds(i * step, step)
        value = part_ref[0, rows].astype(jnp.float32)
        for j in range(1, groups):
            value = value + part_ref[j, rows].astype(jnp.float32)
        value = (value / (1.0 + jnp.exp(-value))).astype(BF)
        for j in range(groups):
            out_ref[j, rows] = value


def hidden_copies(part):
    return pl.pallas_call(
        hidden_kernel,
        out_shape=jax.ShapeDtypeStruct(part.shape, BF),
        in_specs=[INSIDE],
        out_specs=INSIDE,
        compiler_params=pltpu.CompilerParams(vmem_limit_bytes=VMEM),
        cost_estimate=cost(10 * part.size, part, part),
        name="hidden_copies",
    )(part)


def columns_at(weight_ref, place, cols):
    return weight_ref.at[:, pl.ds(pl.multiple_of(place * cols, LANES), cols)]


def down_kernel(x_ref, hidden_ref, weight_ref, w1, w2, w3, out_ref, near, held, near_sems, sems):
    groups, count = hidden_ref.shape[0], held.shape[0]
    step = count // sems.shape[0]
    place = [lax.rem(x_ref[0] + k, groups) for k in range(groups)]
    sources = [columns_at(weight_ref, x_ref[0], near.shape[2]), w1, w2, w3]
    fetches = [pltpu.make_async_copy(source, near.at[k], near_sems.at[k]) for k, source in enumerate(sources)]
    for fetch in fetches:
        fetch.start()
    copies = []

    def part(k, i):
        parts = hidden_ref.shape[1] // count
        lines = [hidden_ref[place[k], pl.ds(h * count + i * step, step)] for h in range(parts)]
        return jnp.dot(jnp.concatenate(lines, axis=1), near[k], preferred_element_type=jnp.float32)

    for i in range(sems.shape[0]):
        rows = pl.ds(i * step, step)
        total = None
        for k in range(groups):
            if i == 0:
                fetches[k].wait()
            total = part(k, i) if k == 0 else total + part(k, i)
        held[rows] = total.astype(BF)
        copies.append(pltpu.make_async_copy(held.at[rows], out_ref.at[rows], sems.at[i]))
        copies[-1].start()
    for copy in copies:
        copy.wait()


def down_rows(x, hidden, weight, after, far, before):
    width, cols = after.shape
    groups, lines, _ = hidden.shape
    out = jax.ShapeDtypeStruct((lines * LANES // width, cols), BF)
    return pl.pallas_call(
        down_kernel,
        out_shape=out,
        in_specs=[pl.BlockSpec(memory_space=pltpu.SMEM), INSIDE] + [OUTSIDE] * 4,
        out_specs=OUTSIDE,
        scratch_shapes=[
            pltpu.VMEM((groups, width, cols), BF),
            pltpu.VMEM(out.shape, BF),
            pltpu.SemaphoreType.DMA((groups,)),
            pltpu.SemaphoreType.DMA((2,)),
        ],
        compiler_params=pltpu.CompilerParams(vmem_limit_bytes=VMEM),
        cost_estimate=cost(2 * hidden.size * cols, hidden, after, after, after, after, out),
        name="down_rows",
    )(x.reshape(1), hidden, weight, after, far, before)


def mix_kernel(take_ref, rows_ref, out_ref, held, sem):
    groups, lines, _ = held.shape
    total = take_ref.shape[0] // 2
    count = total // groups
    mixed = jnp.dot(take_ref[...], rows_ref[...], preferred_element_type=jnp.float32)
    mixed = (mixed[:total] + mixed[total:]).astype(BF)
    for j in range(groups):
        for i in range(lines // count):
            part = mixed[j * count : (j + 1) * count, i * LANES : (i + 1) * LANES]
            held[j, i * count : (i + 1) * count] = part
    copy = pltpu.make_async_copy(held, out_ref, sem)
    copy.start()
    copy.wait()


def mixed_rows(take, rows, groups):
    total, cols = take.shape[0] // 2, rows.shape[1]
    out = jax.ShapeDtypeStruct((groups, total // groups * cols // LANES, LANES), BF)
    return pl.pallas_call(
        mix_kernel,
        out_shape=out,
        in_specs=[INSIDE, INSIDE],
        out_specs=OUTSIDE,
        scratch_shapes=[pltpu.VMEM(out.shape, BF), pltpu.SemaphoreType.DMA(())],
        compiler_params=pltpu.CompilerParams(vmem_limit_bytes=VMEM),
        cost_estimate=cost(2 * take.size * cols, take, rows, out),
        name="mixed_rows",
    )(take, rows)


def sum_kernel(parts_ref, out_ref):
    count = out_ref.shape[0]
    for i in range(out_ref.shape[1] // LANES):
        rows = pl.ds(i * count, count)
        total = parts_ref[0, rows].astype(jnp.float32)
        for j in range(1, parts_ref.shape[0]):
            total = total + parts_ref[j, rows].astype(jnp.float32)
        out_ref[:, i * LANES : (i + 1) * LANES] = total.astype(BF)


def summed(parts, rows, cols):
    out = jax.ShapeDtypeStruct((rows, cols), BF)
    return pl.pallas_call(
        sum_kernel,
        out_shape=out,
        in_specs=[INSIDE],
        out_specs=INSIDE,
        compiler_params=pltpu.CompilerParams(vmem_limit_bytes=VMEM),
        cost_estimate=cost(parts.size, parts, out),
        name="summed",
    )(parts)


def shift(array, by, tp):
    return lax.ppermute(array, "tp", [(i, (i + by) % tp) for i in range(tp)])


def shards(queries, latent_cache, cache_lengths, moe_tokens, expert_ids, gate_scores, up_weight, down_weight):
    tp = lax.axis_size("tp")
    x = lax.axis_index("tp")
    rows, width = moe_tokens.shape
    cols = width // tp
    group = up_weight.shape[2]
    near = lax.axis_size(NEAR)
    away = lax.axis_size(FAR)
    slots = away * CAP

    up = lax.all_to_all(up_weight[0].reshape(tp, cols, group), "tp", 0, 0, tiled=True)

    mine = lax.dynamic_slice_in_dim(moe_tokens, x * cols, cols, 1)
    packed = jnp.concatenate([mine, routing_columns(expert_ids, gate_scores)], axis=1)
    packed = lax.all_gather(packed, FAR, axis=0, tiled=True)
    first = lax.axis_index(FAR) * near
    outgoing = placed_rows(first, packed, rows, near, slots)

    weight = down_weight[0]
    cut = [lax.dynamic_slice_in_dim(weight, (x + k) % tp * cols, cols, 1) for k in (2, 1, tp - 1)]
    outgoing, up, cut = lax.optimization_barrier((outgoing, up, cut))
    far, before, after = (shift(block, k, tp) for block, k in zip(cut, (2, 1, tp - 1)))
    received = lax.all_to_all(outgoing.reshape(near, slots, cols), NEAR, 0, 0, tiled=True)
    received = received.reshape(near * slots, cols)
    take = shares(packed[:, cols:], rows, first, near, away)

    part = up_parts(received, up)
    part, far, after, before = lax.optimization_barrier((part, far, after, before))
    part = lax.all_to_all(part, "tp", 0, 0, tiled=True)
    hidden = lax.all_to_all(hidden_copies(part), "tp", 0, 0, tiled=True)
    output = down_rows(x, hidden, weight, after, far, before)

    returned = lax.all_to_all(output.reshape(near, slots, cols), NEAR, 0, 0, tiled=True)

    asked = [queries] + [shift(queries, k, tp) for k in range(1, tp)]
    own = attend_own(asked, latent_cache, cache_lengths, x * latent_cache.shape[1])
    returned, own = lax.optimization_barrier((returned, own))
    shared = [own[0]] + [shift(own[k], tp - k, tp) for k in range(1, tp)]

    mixed = mixed_rows(take, returned.reshape(near * slots, cols), away)
    mixed = lax.all_to_all(mixed, FAR, 0, 0, tiled=True)
    attention_out = merge(shared)
    expert_mix = summed(mixed, rows, cols)
    return (attention_out, expert_mix)


def solution(mesh):
    devices = mesh.devices
    split = Mesh(devices.reshape(4, 4, 4, 2, devices.shape[1]), EP + ("tp",))
    placed = (
        P(EP, "tp", None),
        P(EP, "tp", None),
        P(EP),
        P(EP, None),
        P(EP, None),
        P(EP, None),
        P(EP, None, "tp"),
        P(EP, "tp", None),
    )
    return jax.shard_map(
        shards,
        mesh=split,
        in_specs=placed,
        out_specs=(P(EP, "tp", None), P(EP, "tp")),
        check_vma=False,
    )
```

```python
import functools

import jax
import jax.numpy as jnp
from jax import lax
from jax.experimental import pallas as pl
from jax.experimental.pallas import tpu as pltpu
from jax.sharding import Mesh, PartitionSpec as P

LATENT = 512
TOP = 8
CAP = 4
SCALE = 192.0 ** (-0.5)
ROUTE_SCALE = 2.5
NEGATIVE = -1e30
LANES = 128
VMEM = 12 << 20
INSIDE = pl.BlockSpec(memory_space=pltpu.VMEM)
OUTSIDE = pl.BlockSpec(memory_space=pltpu.HBM)

EP = ("zh", "zl", "y", "c")
NEAR = ("zl", "y", "c")
FAR = "zh"
BF = jnp.bfloat16


def cost(flops, *arrays):
    size = sum(a.size * a.dtype.itemsize for a in arrays)
    return pl.CostEstimate(flops=flops, bytes_accessed=size, transcendentals=0)


def attend_kernel(place_ref, q0, q1, q2, q3, cache_ref, out_ref):
    r = pl.program_id(0)
    keys = cache_ref[0]
    asked = [q[0] for q in (q0, q1, q2, q3)]
    count = asked[0].shape[0]
    scores = jnp.dot(jnp.concatenate(asked, axis=0), keys, preferred_element_type=jnp.float32) * SCALE
    positions = place_ref[2] + lax.broadcasted_iota(jnp.int32, scores.shape, 1)
    visible = positions < place_ref[r]
    scores = jnp.where(visible, scores, NEGATIVE)
    peak = jnp.max(scores, axis=1, keepdims=True)
    weights = jnp.where(visible, jnp.exp(scores - peak), 0.0)
    total = jnp.sum(weights, axis=1, keepdims=True)
    mixed = lax.dot_general(
        weights.astype(BF), keys[:LATENT], (((1,), (1,)), ((), ())), preferred_element_type=jnp.float32
    )
    mean = (mixed / jnp.where(total > 0.0, total, 1.0)).astype(BF)
    lane = lax.broadcasted_iota(jnp.int32, (scores.shape[0], LANES), 1)
    stats = jnp.zeros((scores.shape[0], LANES), jnp.float32)
    for first, value in ((0, peak), (3, total)):
        for i in range(3):
            part = value.astype(BF).astype(jnp.float32)
            stats = jnp.where(lane == first + i, part, stats)
            value = value - part
    stats = stats.astype(BF)
    for k in range(4):
        out_ref[k, 0, :, :LATENT] = mean[k * count : (k + 1) * count]
        out_ref[k, 0, :, LATENT:] = stats[k * count : (k + 1) * count]


def attend_own(asked, cache, cache_lengths, first):
    keys = jnp.swapaxes(cache, 1, 2)
    count = asked[0].shape[1]
    rows, channels, positions = keys.shape
    out = jax.ShapeDtypeStruct((len(asked), rows, count, LATENT + LANES), BF)
    place = jnp.concatenate([cache_lengths, first.reshape(1).astype(jnp.int32)])
    return pl.pallas_call(
        attend_kernel,
        out_shape=out,
        grid_spec=pltpu.PrefetchScalarGridSpec(
            num_scalar_prefetch=1,
            grid=(rows,),
            in_specs=[pl.BlockSpec((1, count, channels), lambda r, place: (r, 0, 0))] * len(asked)
            + [pl.BlockSpec((1, channels, positions), lambda r, place: (r, 0, 0))],
            out_specs=pl.BlockSpec((len(asked), 1, count, LATENT + LANES), lambda r, place: (0, r, 0, 0)),
        ),
        compiler_params=pltpu.CompilerParams(vmem_limit_bytes=VMEM),
        cost_estimate=cost(4 * rows * 4 * count * channels * positions, cache, out),
        name="attend_own",
    )(place, *asked, keys)


def merge(parts):
    means = [p[..., :LATENT].astype(jnp.float32) for p in parts]
    stats = [p[..., LATENT : LATENT + 6].astype(jnp.float32) for p in parts]
    peaks = [q[..., 0] + q[..., 1] + q[..., 2] for q in stats]
    totals = [q[..., 3] + q[..., 4] + q[..., 5] for q in stats]
    peak = jnp.max(jnp.stack(peaks), axis=0)
    shares = [t * jnp.exp(p - peak) for p, t in zip(peaks, totals)]
    whole = sum(shares)
    return sum((s / whole)[..., None] * m for s, m in zip(shares, means)).astype(BF)


def routing_columns(expert_ids, gate_scores):
    route = gate_scores / jnp.sum(gate_scores, axis=1, keepdims=True) * ROUTE_SCALE
    high = lax.reduce_precision(route, 8, 7)
    low = route - high
    rows = expert_ids.shape[0]
    parts = [expert_ids.astype(BF), high.astype(BF), low.astype(BF)]
    return jnp.concatenate(parts + [jnp.zeros((rows, LANES - 3 * TOP), BF)], axis=1)


def place_kernel(first_ref, packed_ref, out_ref, held, sems, *, rows, experts, slots):
    total, wide = packed_ref.shape
    cols = wide - LANES
    ids = packed_ref[:, cols:].astype(jnp.float32).T
    own = (first_ref[0] + lax.broadcasted_iota(jnp.int32, (experts, total), 0)).astype(jnp.float32)
    named = own == ids[0:1]
    for k in range(1, TOP):
        named = named | (own == ids[k : k + 1])
    before, after = (lax.broadcasted_iota(jnp.int32, (total, total), d) for d in (0, 1))
    earlier = (before < after) & (before // rows == after // rows)
    rank = jnp.dot(
        jnp.where(named, 1.0, 0.0).astype(BF),
        jnp.where(earlier, 1.0, 0.0).astype(BF),
        preferred_element_type=jnp.float32,
    )
    block = lax.broadcasted_iota(jnp.int32, (experts, total), 1) // rows
    slot = jnp.where(named, rank + (block * CAP).astype(jnp.float32), -1.0)
    place = lax.broadcasted_iota(jnp.int32, (experts, slots, total), 1).astype(jnp.float32)
    put = jnp.where(jnp.broadcast_to(slot[:, None, :], place.shape) == place, 1.0, 0.0)
    put = put.reshape(experts * slots, total).astype(BF)
    step = held.shape[0] // sems.shape[0]
    copies = []
    for i in range(sems.shape[0]):
        part = pl.ds(i * step, step)
        moved = jnp.dot(put[i * step : (i + 1) * step], packed_ref[:, :cols], preferred_element_type=jnp.float32)
        held[part] = moved.astype(BF)
        copies.append(pltpu.make_async_copy(held.at[part], out_ref.at[part], sems.at[i]))
        copies[-1].start()
    for copy in copies:
        copy.wait()


def placed_rows(first, packed, rows, experts, slots):
    total, wide = packed.shape
    out = jax.ShapeDtypeStruct((experts * slots, wide - LANES), BF)
    return pl.pallas_call(
        functools.partial(place_kernel, rows=rows, experts=experts, slots=slots),
        out_shape=out,
        in_specs=[pl.BlockSpec(memory_space=pltpu.SMEM), INSIDE],
        out_specs=OUTSIDE,
        scratch_shapes=[pltpu.VMEM(out.shape, BF), pltpu.SemaphoreType.DMA((4,))],
        compiler_params=pltpu.CompilerParams(vmem_limit_bytes=VMEM),
        cost_estimate=cost(2 * out.size * total, packed, out),
        name="placed_rows",
    )(first.reshape(1), packed)


def shares(columns, rows, first, experts, blocks):
    ids = columns[:, :TOP].astype(jnp.float32)
    high = columns[:, TOP : 2 * TOP].astype(jnp.float32)
    low = columns[:, 2 * TOP : 3 * TOP].astype(jnp.float32)
    own = (first + jnp.arange(experts, dtype=jnp.int32)).astype(jnp.float32)
    hit = ids[:, :, None] == own[None, None, :]
    named = jnp.any(hit, axis=1)
    w_high = jnp.sum(jnp.where(hit, high[:, :, None], 0.0), axis=1)
    w_low = jnp.sum(jnp.where(hit, low[:, :, None], 0.0), axis=1)
    total = rows * blocks
    t = jnp.arange(total, dtype=jnp.int32)
    before = (t[None, :] < t[:, None]) & (t[None, :] // rows == t[:, None] // rows)
    rank = jnp.dot(before.astype(BF), named.astype(BF), preferred_element_type=jnp.float32)
    slot = rank + ((t // rows) * CAP).astype(jnp.float32)[:, None]
    slot = jnp.where(named, slot, -1.0)
    slots = jnp.arange(blocks * CAP, dtype=jnp.int32).astype(jnp.float32)
    take = slot[:, :, None] == slots[None, None, :]
    c_high = jnp.where(take, w_high[:, :, None], 0.0).astype(BF).reshape(total, -1)
    c_low = jnp.where(take, w_low[:, :, None], 0.0).astype(BF).reshape(total, -1)
    return jnp.concatenate([c_high, c_low], axis=0)


def up_kernel(rows_ref, weight_ref, out_ref):
    count = rows_ref.shape[0]
    for j in range(weight_ref.shape[0]):
        part = jnp.dot(rows_ref[...], weight_ref[j], preferred_element_type=jnp.float32).astype(BF)
        for i in range(part.shape[1] // LANES):
            out_ref[j, i * count : (i + 1) * count] = part[:, i * LANES : (i + 1) * LANES]


def up_parts(rows, weight):
    groups, depth, width = weight.shape
    count = rows.shape[0]
    out = jax.ShapeDtypeStruct((groups, count * width // LANES, LANES), BF)
    return pl.pallas_call(
        up_kernel,
        out_shape=out,
        in_specs=[INSIDE, INSIDE],
        out_specs=INSIDE,
        compiler_params=pltpu.CompilerParams(vmem_limit_bytes=VMEM),
        cost_estimate=cost(2 * count * depth * width * groups, rows, weight, out),
        name="up_parts",
    )(rows, weight)


def hidden_kernel(part_ref, out_ref):
    groups, count, _ = part_ref.shape
    step = count // 4
    for i in range(4):
        rows = pl.ds(i * step, step)
        value = part_ref[0, rows].astype(jnp.float32)
        for j in range(1, groups):
            value = value + part_ref[j, rows].astype(jnp.float32)
        value = (value / (1.0 + jnp.exp(-value))).astype(BF)
        for j in range(groups):
            out_ref[j, rows] = value


def hidden_copies(part):
    return pl.pallas_call(
        hidden_kernel,
        out_shape=jax.ShapeDtypeStruct(part.shape, BF),
        in_specs=[INSIDE],
        out_specs=INSIDE,
        compiler_params=pltpu.CompilerParams(vmem_limit_bytes=VMEM),
        cost_estimate=cost(10 * part.size, part, part),
        name="hidden_copies",
    )(part)


def columns_at(weight_ref, place, cols):
    return weight_ref.at[:, pl.ds(pl.multiple_of(place * cols, LANES), cols)]


def down_kernel(x_ref, hidden_ref, weight_ref, w1, low, high, w3, out_ref, near, held, near_sems, sems):
    groups, count = hidden_ref.shape[0], held.shape[0]
    step = count // sems.shape[0]
    place = [lax.rem(x_ref[0] + k, groups) for k in range(groups)]
    half = low.shape[0]
    own = columns_at(weight_ref, x_ref[0], near.shape[2])
    parts = [(own, near.at[0]), (w1, near.at[1]), (w3, near.at[3])]
    parts = parts + [(low, near.at[2, pl.ds(0, half)]), (high, near.at[2, pl.ds(half, half)])]
    fetches = [pltpu.make_async_copy(*pair, near_sems.at[i]) for i, pair in enumerate(parts)]
    for fetch in fetches:
        fetch.start()
    copies = []

    def part(k, i):
        parts = hidden_ref.shape[1] // count
        lines = [hidden_ref[place[k], pl.ds(h * count + i * step, step)] for h in range(parts)]
        return jnp.dot(jnp.concatenate(lines, axis=1), near[k], preferred_element_type=jnp.float32)

    for i in range(sems.shape[0]):
        rows = pl.ds(i * step, step)
        total = None
        for step_at, k in enumerate((0, 1, 3, 2)):
            if i == 0:
                for fetch in fetches[step_at:] if k == 2 else fetches[step_at : step_at + 1]:
                    fetch.wait()
            total = part(k, i) if k == 0 else total + part(k, i)
        held[rows] = total.astype(BF)
        copies.append(pltpu.make_async_copy(held.at[rows], out_ref.at[rows], sems.at[i]))
        copies[-1].start()
    for copy in copies:
        copy.wait()


def down_rows(x, hidden, weight, after, low, high, before):
    width, cols = after.shape
    groups, lines, _ = hidden.shape
    out = jax.ShapeDtypeStruct((lines * LANES // width, cols), BF)
    return pl.pallas_call(
        down_kernel,
        out_shape=out,
        in_specs=[pl.BlockSpec(memory_space=pltpu.SMEM), INSIDE] + [OUTSIDE] * 5,
        out_specs=OUTSIDE,
        scratch_shapes=[
            pltpu.VMEM((groups, width, cols), BF),
            pltpu.VMEM(out.shape, BF),
            pltpu.SemaphoreType.DMA((groups + 1,)),
            pltpu.SemaphoreType.DMA((2,)),
        ],
        compiler_params=pltpu.CompilerParams(vmem_limit_bytes=VMEM),
        cost_estimate=cost(2 * hidden.size * cols, hidden, after, after, after, after, out),
        name="down_rows",
    )(x.reshape(1), hidden, weight, after, low, high, before)


def mix_kernel(take_ref, rows_ref, out_ref, held, sem):
    groups, lines, _ = held.shape
    total = take_ref.shape[0] // 2
    count = total // groups
    mixed = jnp.dot(take_ref[...], rows_ref[...], preferred_element_type=jnp.float32)
    mixed = (mixed[:total] + mixed[total:]).astype(BF)
    for j in range(groups):
        for i in range(lines // count):
            part = mixed[j * count : (j + 1) * count, i * LANES : (i + 1) * LANES]
            held[j, i * count : (i + 1) * count] = part
    copy = pltpu.make_async_copy(held, out_ref, sem)
    copy.start()
    copy.wait()


def mixed_rows(take, rows, groups):
    total, cols = take.shape[0] // 2, rows.shape[1]
    out = jax.ShapeDtypeStruct((groups, total // groups * cols // LANES, LANES), BF)
    return pl.pallas_call(
        mix_kernel,
        out_shape=out,
        in_specs=[INSIDE, INSIDE],
        out_specs=OUTSIDE,
        scratch_shapes=[pltpu.VMEM(out.shape, BF), pltpu.SemaphoreType.DMA(())],
        compiler_params=pltpu.CompilerParams(vmem_limit_bytes=VMEM),
        cost_estimate=cost(2 * take.size * cols, take, rows, out),
        name="mixed_rows",
    )(take, rows)


def sum_kernel(parts_ref, out_ref):
    count = out_ref.shape[0]
    for i in range(out_ref.shape[1] // LANES):
        rows = pl.ds(i * count, count)
        total = parts_ref[0, rows].astype(jnp.float32)
        for j in range(1, parts_ref.shape[0]):
            total = total + parts_ref[j, rows].astype(jnp.float32)
        out_ref[:, i * LANES : (i + 1) * LANES] = total.astype(BF)


def summed(parts, rows, cols):
    out = jax.ShapeDtypeStruct((rows, cols), BF)
    return pl.pallas_call(
        sum_kernel,
        out_shape=out,
        in_specs=[INSIDE],
        out_specs=INSIDE,
        compiler_params=pltpu.CompilerParams(vmem_limit_bytes=VMEM),
        cost_estimate=cost(parts.size, parts, out),
        name="summed",
    )(parts)


def shift(array, by, tp):
    return lax.ppermute(array, "tp", [(i, (i + by) % tp) for i in range(tp)])


def shards(queries, latent_cache, cache_lengths, moe_tokens, expert_ids, gate_scores, up_weight, down_weight):
    tp = lax.axis_size("tp")
    x = lax.axis_index("tp")
    rows, width = moe_tokens.shape
    cols = width // tp
    group = up_weight.shape[2]
    near = lax.axis_size(NEAR)
    away = lax.axis_size(FAR)
    slots = away * CAP

    up = lax.all_to_all(up_weight[0].reshape(tp, cols, group), "tp", 0, 0, tiled=True)

    mine = lax.dynamic_slice_in_dim(moe_tokens, x * cols, cols, 1)
    packed = jnp.concatenate([mine, routing_columns(expert_ids, gate_scores)], axis=1)
    packed = lax.all_gather(packed, FAR, axis=0, tiled=True)
    first = lax.axis_index(FAR) * near
    outgoing = placed_rows(first, packed, rows, near, slots)

    weight = down_weight[0]
    half = group // 2

    def columns_for(k, first_row, count):
        return lax.dynamic_slice(weight, (first_row, (x + k) % tp * cols), (count, cols))

    cut = [columns_for(2, 0, half), columns_for(2, half, half), columns_for(1, 0, group), columns_for(tp - 1, 0, group)]
    outgoing, up, cut = lax.optimization_barrier((outgoing, up, cut))
    low, high = shift(cut[0], 1, tp), shift(cut[1], tp - 1, tp)
    before, after = shift(cut[2], 1, tp), shift(cut[3], tp - 1, tp)
    low, high = shift(low, 1, tp), shift(high, tp - 1, tp)
    received = lax.all_to_all(outgoing.reshape(near, slots, cols), NEAR, 0, 0, tiled=True)
    received = received.reshape(near * slots, cols)
    take = shares(packed[:, cols:], rows, first, near, away)

    part = up_parts(received, up)
    part, low, high, after, before = lax.optimization_barrier((part, low, high, after, before))
    part = lax.all_to_all(part, "tp", 0, 0, tiled=True)
    hidden = lax.all_to_all(hidden_copies(part), "tp", 0, 0, tiled=True)
    output = down_rows(x, hidden, weight, after, low, high, before)

    returned = lax.all_to_all(output.reshape(near, slots, cols), NEAR, 0, 0, tiled=True)

    asked = [queries] + [shift(queries, k, tp) for k in range(1, tp)]
    own = attend_own(asked, latent_cache, cache_lengths, x * latent_cache.shape[1])
    returned, own = lax.optimization_barrier((returned, own))
    shared = [own[0]] + [shift(own[k], tp - k, tp) for k in range(1, tp)]

    mixed = mixed_rows(take, returned.reshape(near * slots, cols), away)
    mixed = lax.all_to_all(mixed, FAR, 0, 0, tiled=True)
    attention_out = merge(shared)
    expert_mix = summed(mixed, rows, cols)
    return (attention_out, expert_mix)


def solution(mesh):
    devices = mesh.devices
    split = Mesh(devices.reshape(4, 4, 4, 2, devices.shape[1]), EP + ("tp",))
    placed = (
        P(EP, "tp", None),
        P(EP, "tp", None),
        P(EP),
        P(EP, None),
        P(EP, None),
        P(EP, None),
        P(EP, None, "tp"),
        P(EP, "tp", None),
    )
    return jax.shard_map(
        shards,
        mesh=split,
        in_specs=placed,
        out_specs=(P(EP, "tp", None), P(EP, "tp")),
        check_vma=False,
    )
```
